512 devices in a mesh: row: 128 (over x, y_lo, z), rep: 4 (over y_hi, core).
Axes of the slice: x: 4, y: 8 (y_hi: 2, y_lo: 4; y = y_hi * 4 + y_lo), z: 8, core: 2. Of those that a mesh axis runs over, the one named last changes fastest.
Arguments:
- pair: bfloat16 [2048, 512, 128], P(('rep', 'row')), parts along dimension 0, may hold values from -6 to 6
- token_mask: int32 [2048], P('rep'), parts along dimension 0, may hold values from 0 to 1, as said below
- start_gain: float32 [128], replicated, may hold values from 0.5 to 1.5
- start_proj: bfloat16 [128, 512], replicated, may hold values from -1 to 1
- start_bias: bfloat16 [128, 4], replicated, may hold values from -0.5 to 0.5
- start_out: bfloat16 [128, 128], replicated, may hold values from -0.5 to 0.5
- end_gain: float32 [128], replicated, may hold values from 0.5 to 1.5
- end_proj: bfloat16 [128, 512], replicated, may hold values from -1 to 1
- end_bias: bfloat16 [128, 4], replicated, may hold values from -0.5 to 0.5
- end_out: bfloat16 [128, 128], replicated, may hold values from -0.5 to 0.5
Outputs:
- updated: bfloat16 [2048, 512, 128], P(('rep', 'row')), parts along dimension 0
The draws below stay inside these ranges and needn't reach their ends.
There are 4 independent parts, one for each index of `rep`. The reference program is written for one: setup_inputs(seed, part) draws one part's arguments, and reference() takes and returns one part's arrays. A program takes and returns all parts, laid end to end along the dimension named above; an argument that names none is the same for every part. Nothing has to cross between parts.
Inputs may be any that keep to these rules, and one draw needn't show every extreme that they name: `token_mask`: exactly 448 entries are 1, at positions drawn from the seed.
All inputs are finite; a program needn't handle non-finite values.
Results may differ from the reference program's by a relative error of at most 0.006.
Values may be sent and summed in bfloat16 or wider, within the bound.
A program may use at most 64 MiB of HBM per device.

```python
import math
import jax
import jax.numpy as jnp
from jax import lax

C = 128
HEADS = 4
N_RES = 512


def draw_token_mask(key, part):
    key = jax.random.fold_in(key, 11)
    order = jax.random.permutation(key, N_RES)
    return (order < N_RES - N_RES // 8).astype(jnp.int32)


def draw_pair(key, part):
    key = jax.random.fold_in(key, 21)
    return jnp.clip(jax.random.normal(key, (N_RES, N_RES, C), jnp.float32), -6.0, 6.0).astype(jnp.bfloat16)


def draw_start_proj(key, part):
    key = jax.random.fold_in(key, 31)
    return (jnp.clip(jax.random.normal(key, (C, 4 * C), jnp.float32), -4.0, 4.0) / math.sqrt(C)).astype(jnp.bfloat16)


def draw_end_proj(key, part):
    key = jax.random.fold_in(key, 41)
    return (jnp.clip(jax.random.normal(key, (C, 4 * C), jnp.float32), -4.0, 4.0) / math.sqrt(C)).astype(jnp.bfloat16)


def scatter_about(rng, shape, scale, bound, held_as=jnp.bfloat16):
    values = scale * jax.random.normal(rng, shape, jnp.float32)
    return jnp.clip(values, min=-bound, max=bound).astype(held_as)


def setup_inputs(seed: int = 0, part: int = 0) -> dict:
    splits = jax.random.split(jax.random.key(seed), 11)
    own_keys = jax.random.split(jax.random.fold_in(splits[10], part), 11)
    pair = draw_pair(jax.random.fold_in(jax.random.fold_in(splits[10], part), 71), part)
    token_mask = draw_token_mask(jax.random.fold_in(jax.random.fold_in(splits[10], part), 71), part)
    start_gain = jnp.clip(1.0 + 0.1 * jax.random.normal(splits[2], (C,), jnp.float32), 0.5, 1.5)
    start_proj = draw_start_proj(jax.random.fold_in(splits[10], 71), part)
    start_bias = scatter_about(splits[4], (C, HEADS), C ** -0.5, 0.5)
    start_out = scatter_about(splits[5], (C, C), C ** -0.5, 0.5)
    end_gain = jnp.clip(1.0 + 0.1 * jax.random.normal(splits[6], (C,), jnp.float32), 0.5, 1.5)
    end_proj = draw_end_proj(jax.random.fold_in(splits[10], 71), part)
    end_bias = scatter_about(splits[8], (C, HEADS), C ** -0.5, 0.5)
    end_out = scatter_about(splits[9], (C, C), C ** -0.5, 0.5)
    return dict(pair=pair, token_mask=token_mask, start_gain=start_gain, start_proj=start_proj, start_bias=start_bias, start_out=start_out, end_gain=end_gain, end_proj=end_proj, end_bias=end_bias, end_out=end_out)


def layer_norm(values, gain):
    wide = values.astype(jnp.float32)
    center = wide - lax.optimization_barrier(jnp.mean(wide, axis=-1, keepdims=True))
    spread = lax.optimization_barrier(jnp.mean(center * center, axis=-1, keepdims=True))
    return (center * lax.rsqrt(spread + 1e-05) * gain).astype(jnp.bfloat16)

def triangle_update(table, mask_term, gain, w_proj, w_bias, w_out):
    count = table.shape[0]
    width = w_out.shape[0]
    heads = w_bias.shape[1]
    head_size = width // heads
    scale = 1.0 / math.sqrt(head_size)
    normed = layer_norm(table, gain)
    bias_full = jnp.einsum('jkc,ch->hjk', normed.astype(jnp.float32), w_bias.astype(jnp.float32)).astype(jnp.bfloat16)

    def rows_fn(block):
        strip = lax.dynamic_slice_in_dim(normed, block * 8, 8, 0)
        proj = jnp.dot(strip, w_proj, preferred_element_type=jnp.float32).astype(jnp.bfloat16)
        query = proj[:, :, :width].reshape(8, count, heads, head_size).astype(jnp.float32)
        keys = proj[:, :, width:2 * width].reshape(8, count, heads, head_size).astype(jnp.float32)
        values = proj[:, :, 2 * width:3 * width].reshape(8, count, heads, head_size).astype(jnp.float32)
        gates = proj[:, :, 3 * width:].astype(jnp.float32)
        scores = jnp.einsum('rjhd,rkhd->rhjk', query, keys) * scale
        scores = scores + bias_full.astype(jnp.float32)[None] + mask_term
        scores = scores - lax.optimization_barrier(jnp.max(scores, axis=-1, keepdims=True))
        expo = jnp.exp(scores)
        probs = (expo / lax.optimization_barrier(jnp.sum(expo, axis=-1, keepdims=True))).astype(jnp.bfloat16)
        attended = jnp.einsum('rhjk,rkhd->rjhd', probs.astype(jnp.float32), values).reshape(8, count, width)
        hidden = (jax.nn.sigmoid(gates) * attended).astype(jnp.bfloat16)
        return jnp.dot(hidden, w_out, preferred_element_type=jnp.float32)
    blocks = lax.map(rows_fn, jnp.arange(count // 8, dtype=jnp.int32))
    return blocks.reshape(count, count, width)

def reference(pair, token_mask, start_gain, start_proj, start_bias, start_out, end_gain, end_proj, end_bias, end_out):
    mask_term = (token_mask.astype(jnp.float32) - 1.0) * 1000000000.0
    first = (pair.astype(jnp.float32) + triangle_update(pair, mask_term, start_gain, start_proj, start_bias, start_out)).astype(jnp.bfloat16)
    flipped = jnp.swapaxes(first, 0, 1)
    late = triangle_update(flipped, mask_term, end_gain, end_proj, end_bias, end_out).astype(jnp.bfloat16)
    return (first.astype(jnp.float32) + jnp.swapaxes(late, 0, 1).astype(jnp.float32)).astype(jnp.bfloat16)
```

```python
import functools
import math

import jax
import jax.numpy as jnp
from jax import lax
from jax.experimental import pallas as pl
from jax.experimental.pallas import tpu as pltpu
from jax.sharding import PartitionSpec as P

MESH = pl.DeviceIdType.MESH
LOG2E = 1.4426950408889634
F32 = jnp.float32
BF16 = jnp.bfloat16
ROWS = 4
HEADS = 4
CH = ROWS * HEADS


def iota(shape, dim):
    return lax.broadcasted_iota(jnp.int32, shape, dim)


def nt(a, b):
    return lax.dot_general(a, b, (((1,), (1,)), ((), ())), preferred_element_type=F32)


def mm(a, b):
    return jnp.dot(a, b, preferred_element_type=F32)


def ln(wide, gain):
    center = wide - jnp.mean(wide, axis=-1, keepdims=True)
    spread = jnp.mean(center * center, axis=-1, keepdims=True)
    return (center * lax.rsqrt(spread + 1e-05) * gain).astype(BF16)


def kernel(
    dims, nb,
    pair_ref, mask_ref, sg_ref, sp_ref, sb_ref, so_ref, eg_ref, ep_ref, eb_ref, eo_ref,
    out_ref,
    x_s, q_s, k_s, v_s, g_s, first_s, bias0_s, bias1_s, stage0_s, stage1_s, recv0_s, recv1_s,
    spread_s, fold_s, head_s, send_perm_s, recv_perm_s,
    z_send, z_recv, y_send, y_recv, x_send, x_recv, a_send, a_recv,
):
    nx, ny, nz = dims
    n = nx * ny * nz
    me = lax.axis_index("row")
    x, y, z = me // (ny * nz), (me // nz) % ny, me % nz
    width = x_s.shape[2]
    size = width // HEADS
    blk = nb * ROWS
    tall = blk * HEADS

    barrier = pltpu.get_barrier_semaphore()

    def greet(s, c):
        pl.semaphore_signal(
            barrier, inc=1, device_id={"row": lax.rem(me + s, n)}, device_id_type=MESH
        )
        return c

    lax.fori_loop(1, n, greet, 0)

    def chunk(ref, first, count):
        return ref.at[pl.ds(pl.multiple_of(first * CH, CH), count * CH)]

    def remote(src, dst, send, recv, peer):
        return pltpu.make_async_remote_copy(
            src_ref=src, dst_ref=dst, send_sem=send, recv_sem=recv,
            device_id={"row": peer}, device_id_type=MESH,
        )

    def wait_bytes(ref, count, sem):
        view = ref.at[pl.ds(0, count * CH)]
        pltpu.make_async_copy(view, view, sem).wait()

    spread_s[...] = (iota((tall, blk), 0) // HEADS == iota((tall, blk), 1)).astype(F32).astype(BF16)
    fold_s[...] = (iota((blk, tall), 1) // HEADS == iota((blk, tall), 0)).astype(F32).astype(BF16)
    head_s[...] = (iota((tall, width), 0) % HEADS == iota((tall, width), 1) // size).astype(F32)
    o, i = iota((tall, tall), 0), iota((tall, tall), 1)
    send_perm_s[...] = (
        (o % ROWS) * blk + (o // CH) * ROWS + (o // ROWS) % ROWS == i
    ).astype(F32).astype(BF16)
    recv_perm_s[...] = (
        ((o // ROWS) % nb) * CH + (o // blk) * ROWS + o % ROWS == i
    ).astype(F32).astype(BF16)
    mask_term = (mask_ref[...].astype(F32) - 1.0) * (1e9 * LOG2E)
    v_s[:, :, width:] = jnp.ones((ROWS, v_s.shape[1], width), BF16)

    def share_of_bias(b_ref):
        total = None
        for r in range(ROWS):
            row, col = iota((CH, HEADS), 0), iota((CH, HEADS), 1)
            pick = ((row // HEADS == r) & (row % HEADS == col)).astype(F32).astype(BF16)
            term = nt(nt(pick, b_ref[...]).astype(BF16), x_s[r])
            total = term if total is None else total + term
        return (total * LOG2E + mask_term).astype(BF16)

    def gather_z(t, bias):
        def go(s, c):
            peer = me - z + lax.rem(z + s, nz)
            mine = chunk(bias, me, 1)
            remote(mine, mine, z_send.at[t], z_recv.at[t], peer).start()
            return c

        lax.fori_loop(1, nz, go, 0)

    def gather_y(t, bias):
        wait_bytes(bias, nz - 1, z_recv.at[t])

        def go(s, c):
            peer = me + (lax.rem(y + s, ny) - y) * nz
            line = chunk(bias, me - z, nz)
            remote(line, line, y_send.at[t], y_recv.at[t], peer).start()
            return c

        lax.fori_loop(1, ny, go, 0)

    def gather_x(t, bias):
        wait_bytes(bias, (ny - 1) * nz, y_recv.at[t])
        for s in range(1, nx):
            peer = me + (lax.rem(x + s, nx) - x) * (ny * nz)
            plane = chunk(bias, x * (ny * nz), ny * nz)
            remote(plane, plane, x_send.at[t, s], x_recv.at[t, nx - s], peer).start()

    def project(p_ref):
        for r in range(ROWS):
            out = mm(x_s[r], p_ref[...])
            q_s[r] = (out[:, :width] * (LOG2E / math.sqrt(size))).astype(BF16)
            k_s[r] = out[:, width : 2 * width].astype(BF16)
            v_s[r, :, :width] = out[:, 2 * width : 3 * width].astype(BF16)
            gate = out[:, 3 * width :].astype(BF16).astype(F32)
            g_s[r] = jax.nn.sigmoid(gate)

    def attend(t, bias, o_ref, stage, recv, residual):
        per_plane = ny * nz // nb

        def block(p, c):
            step, half = p // per_plane, p % per_plane
            rel = step ^ (step >> 1)
            plane = lax.rem(x + rel, nx)

            @pl.when((half == 0) & (step > 0))
            def _():
                wait_bytes(bias, ny * nz, x_recv.at[t, rel])

            b = plane * per_plane + lax.rem(half + y * per_plane // ny, per_plane)
            rows = pl.ds(pl.multiple_of(b * tall, tall), tall)
            here = pl.ds(pl.multiple_of(b * blk, blk), blk)
            done = []
            for r in range(ROWS):
                q = (mm(spread_s[...], q_s[r, here, :]) * head_s[...]).astype(BF16)
                s = nt(q, k_s[r]) + bias[rows, :].astype(F32)
                e = jnp.exp2(s - jnp.max(s, axis=-1, keepdims=True)).astype(BF16)
                a = mm(e, v_s[r])
                a = (a[:, :width] * (head_s[...] / a[:, width:])).astype(BF16)
                h = (g_s[r, here, :] * mm(fold_s[...], a)).astype(BF16)
                u = mm(h, o_ref[...])
                if residual is not None:
                    u = residual[r, here, :].astype(F32) + u
                u = u.astype(BF16)
                if residual is not None:
                    first_s[r, here, :] = u
                done.append(u)
            stage[rows, :] = mm(send_perm_s[...], jnp.concatenate(done, axis=0)).astype(BF16)

            def send(k, c):
                peer = b * nb + lax.rem(me + k, nb)

                @pl.when(peer != me)
                def _():
                    remote(
                        chunk(stage, peer, 1), chunk(recv, me, 1), a_send.at[t], a_recv.at[t], peer
                    ).start()

                return c

            lax.fori_loop(0, nb, send, 0)
            return c

        lax.fori_loop(0, n // nb, block, 0)
        mine = pl.ds(pl.multiple_of(me * CH, CH), CH)
        recv[mine, :] = stage[mine, :]
        wait_bytes(recv, n - 1, a_recv.at[t])

    def drain(t, bias, stage):
        wait_bytes(bias, nz - 1, z_send.at[t])
        wait_bytes(bias, (ny - 1) * nz, y_send.at[t])
        for s in range(1, nx):
            wait_bytes(bias, ny * nz, x_send.at[t, s])
        wait_bytes(stage, n - 1, a_send.at[t])

    def update(t, g_ref, p_ref, b_ref, o_ref, bias, stage, recv, residual):
        bias[pl.ds(pl.multiple_of(me * CH, CH), CH), :] = share_of_bias(b_ref)
        if t == 0:
            pl.semaphore_wait(barrier, n - 1)
        gather_z(t, bias)
        project(p_ref)
        gather_y(t, bias)
        gather_x(t, bias)
        attend(t, bias, o_ref, stage, recv, residual)

    for r in range(ROWS):
        x_s[r] = ln(pair_ref[r].astype(F32), sg_ref[...])
    update(0, sg_ref, sp_ref, sb_ref, so_ref, bias0_s, stage0_s, recv0_s, pair_ref)

    def norm_block(b, c):
        rows = pl.ds(pl.multiple_of(b * tall, tall), tall)
        here = pl.ds(pl.multiple_of(b * blk, blk), blk)
        normed = ln(mm(recv_perm_s[...], recv0_s[rows, :]), eg_ref[...])
        for u in range(ROWS):
            x_s[u, here, :] = normed[u * blk : (u + 1) * blk]
        return c

    lax.fori_loop(0, n // nb, norm_block, 0)
    update(1, eg_ref, ep_ref, eb_ref, eo_ref, bias1_s, stage1_s, recv1_s, None)

    def last_block(b, c):
        rows = pl.ds(pl.multiple_of(b * tall, tall), tall)
        here = pl.ds(pl.multiple_of(b * blk, blk), blk)
        late = mm(recv_perm_s[...], recv1_s[rows, :])
        for u in range(ROWS):
            out_ref[u, here, :] = (
                first_s[u, here, :].astype(F32) + late[u * blk : (u + 1) * blk]
            ).astype(BF16)
        return c

    lax.fori_loop(0, n // nb, last_block, 0)
    drain(0, bias0_s, stage0_s)
    drain(1, bias1_s, stage1_s)


def dims_of(n):
    return (4, 4, 8) if n == 128 else (2, 2, n // 4)


def solution(mesh):
    n = mesh.shape["row"]
    dims = dims_of(n)
    nb = min(16, dims[1] * dims[2] // 2)

    def body(pair, token_mask, sg, sp, sb, so, eg, ep, eb, eo):
        rows, count, width = pair.shape
        tall, blk = nb * CH, nb * ROWS
        vmem = pl.BlockSpec(memory_space=pltpu.VMEM)
        dma = pltpu.SemaphoreType.DMA
        return pl.pallas_call(
            functools.partial(kernel, dims, nb),
            out_shape=jax.ShapeDtypeStruct(pair.shape, BF16),
            in_specs=[vmem] * 10,
            out_specs=vmem,
            scratch_shapes=[
                pltpu.VMEM((rows, count, width), BF16),
                pltpu.VMEM((rows, count, width), BF16),
                pltpu.VMEM((rows, count, width), BF16),
                pltpu.VMEM((rows, count, 2 * width), BF16),
                pltpu.VMEM((rows, count, width), F32),
                pltpu.VMEM((rows, count, width), BF16),
                pltpu.VMEM((n * CH, count), BF16),
                pltpu.VMEM((n * CH, count), BF16),
                pltpu.VMEM((n * CH, width), BF16),
                pltpu.VMEM((n * CH, width), BF16),
                pltpu.VMEM((n * CH, width), BF16),
                pltpu.VMEM((n * CH, width), BF16),
                pltpu.VMEM((tall, blk), BF16),
                pltpu.VMEM((blk, tall), BF16),
                pltpu.VMEM((tall, width), F32),
                pltpu.VMEM((tall, tall), BF16),
                pltpu.VMEM((tall, tall), BF16),
                dma((2,)), dma((2,)), dma((2,)), dma((2,)),
                dma((2, dims[0])), dma((2, dims[0])), dma((2,)), dma((2,)),
            ],
            compiler_params=pltpu.CompilerParams(
                collective_id=0, has_side_effects=True, vmem_limit_bytes=56 * 1024 * 1024
            ),
        )(
            pair, token_mask.reshape(1, count), sg.reshape(1, width), sp, sb, so,
            eg.reshape(1, width), ep, eb, eo,
        )

    return jax.shard_map(
        body,
        mesh=mesh,
        in_specs=(P(("rep", "row"), None, None), P("rep"), P(), P(), P(), P(), P(), P(), P(), P()),
        out_specs=P(("rep", "row"), None, None),
        check_vma=False,
    )
```

```python
import functools
import math

import jax
import jax.numpy as jnp
from jax import lax
from jax.experimental import pallas as pl
from jax.experimental.pallas import tpu as pltpu
from jax.sharding import PartitionSpec as P

MESH = pl.DeviceIdType.MESH
LOG2E = 1.4426950408889634
F32 = jnp.float32
BF16 = jnp.bfloat16
ROWS = 4
TEAM = 2 * ROWS
HEADS = 4
CH = ROWS * HEADS


def iota(shape, dim):
    return lax.broadcasted_iota(jnp.int32, shape, dim)


def one_hot(cond):
    return cond.astype(F32).astype(BF16)


def nt(a, b):
    return lax.dot_general(a, b, (((1,), (1,)), ((), ())), preferred_element_type=F32)


def mm(a, b):
    return jnp.dot(a, b, preferred_element_type=F32)


def ln(wide, gain):
    center = wide - jnp.mean(wide, axis=-1, keepdims=True)
    spread = jnp.mean(center * center, axis=-1, keepdims=True)
    return (center * lax.rsqrt(spread + 1e-05) * gain).astype(BF16)


def kernel(
    dims,
    pair_ref, mask_ref, sg_ref, sp_ref, sb_ref, so_ref, eg_ref, ep_ref, eb_ref, eo_ref,
    out_ref,
    raw0_s, raw1_s, x_s, v_s, score_s, gate_s, res_s, e_s, top_s, low_s, turn_s,
    bias0_s, bias1_s, stage0_s, stage1_s, recv0_s, recv1_s, pick_s, spread_s, wkv_s, wqg_s,
    t_send, t_recv, y_send, y_recv, z_send, z_recv, x_send, x_recv, a_send, a_recv,
):
    nx, ny, nz = dims
    nzi = nz // 2
    per = ny * nzi
    members = nx * per
    me = lax.axis_index("row")
    cls, mine = me % 2, me // 2
    x, y, zi = mine // per, (mine // nzi) % ny, mine % nzi
    width = x_s.shape[2]
    count = x_s.shape[1]
    size = width // HEADS
    quer = per * ROWS
    tall = quer * HEADS
    span = per * TEAM

    barrier = pltpu.get_barrier_semaphore()

    def greet_one(peer):
        pl.semaphore_signal(barrier, inc=1, device_id={"row": peer}, device_id_type=MESH)

    def member(m):
        return 2 * m + cls

    partner = me + 1 - 2 * cls
    greet_one(partner)

    def greet(s, c):
        greet_one(member(lax.rem(mine + s, members)))
        return c

    lax.fori_loop(1, members, greet, 0)

    def remote(src, dst, send, recv, peer):
        return pltpu.make_async_remote_copy(
            src_ref=src, dst_ref=dst, send_sem=send, recv_sem=recv,
            device_id={"row": peer}, device_id_type=MESH,
        )

    def wait_for(view, sem):
        pltpu.make_async_copy(view, view, sem).wait()

    row, col = iota((quer, span), 0), iota((quer, span), 1)
    pick_s[...] = one_hot((row // ROWS) * TEAM + ROWS * cls + row % ROWS == col)
    spread_s[...] = one_hot(iota((tall, quer), 0) // HEADS == iota((tall, quer), 1))
    lane_head = iota((quer, width), 1) // size
    head = (iota((tall, width), 0) % HEADS == iota((tall, width), 1) // size).astype(F32)
    mask_term = (mask_ref[...].astype(F32) - 1.0) * (1e9 * LOG2E)
    v_s[:, :, width:] = jnp.ones((TEAM, count, width), BF16)

    own = ROWS * cls
    other = ROWS - own

    def update(t, g_ref, p_ref, b_ref, o_ref, raw, bias, stage, recv, rounded):
        own_rows = raw.at[pl.ds(own, ROWS)]
        remote(own_rows, own_rows, t_send.at[t], t_recv.at[t], partner).start()

        total = None
        for r in range(ROWS):
            normed = ln(raw[own + r].astype(F32), g_ref[...])
            x_s[own + r] = normed
            a, b = iota((CH, HEADS), 0), iota((CH, HEADS), 1)
            pick = one_hot((a // HEADS == r) & (a % HEADS == b))
            term = nt(mm(pick, b_ref[...]).astype(BF16), normed)
            total = term if total is None else total + term
        bias[x, y, zi] = (total * LOG2E + mask_term).astype(BF16)

        def send_y(s, c):
            peer = member(mine + (lax.rem(y + s, ny) - y) * nzi)
            share = bias.at[x, y, zi]
            remote(share, share, y_send.at[t], y_recv.at[t], peer).start()
            return c

        lax.fori_loop(1, ny, send_y, 0)

        wkv_s[...] = p_ref[:, width : 3 * width]
        wqg_s[:, :width] = p_ref[:, :width]
        wqg_s[:, width:] = p_ref[:, 3 * width :]

        def project(i, c):
            normed = x_s[i]
            kv = mm(normed, wkv_s[...])
            keys = kv[:, :width].astype(BF16)
            v_s[i, :, :width] = kv[:, width:].astype(BF16)
            for p in range(nx):
                part = slice(p * span, (p + 1) * span)
                here = slice(p * quer, (p + 1) * quer)
                both = jnp.concatenate([normed[part], raw[i, part, :]], axis=1)
                both = mm(pick_s[...], both)
                res_s[i, here, :] = both[:, width:]
                qg = mm(both[:, :width].astype(BF16), wqg_s[...])
                gate_s[i, here, :] = jax.nn.sigmoid(qg[:, width:].astype(BF16).astype(F32))
                q = (qg[:, :width] * (LOG2E / math.sqrt(size))).astype(BF16)
                q = (mm(spread_s[...], q) * head).astype(BF16)
                score_s[i, p] = nt(q, keys)
            return c

        lax.fori_loop(own, own + 2, project, 0)

        if ny > 1:
            wait_for(bias.at[0, pl.ds(0, ny - 1), 0], y_recv.at[t])

        def send_z(s, c):
            peer = member(mine + lax.rem(zi + s, nzi) - zi)
            line = bias.at[x, :, zi]
            remote(line, line, z_send.at[t], z_recv.at[t], peer).start()
            return c

        lax.fori_loop(1, nzi, send_z, 0)
        lax.fori_loop(own + 2, own + ROWS, project, 0)
        wait_for(bias.at[0, :, pl.ds(0, nzi - 1)], z_recv.at[t])

        up, down = lax.rem(x + 1, nx), lax.rem(x + nx - 1, nx)
        far = lax.rem(x + 2, nx)
        to_up = member(mine + (up - x) * per)
        to_down = member(mine + (down - x) * per)
        remote(bias.at[x], bias.at[x], x_send.at[t], x_recv.at[t, 1], to_up).start()
        remote(bias.at[x], bias.at[x], x_send.at[t], x_recv.at[t, 0], to_down).start()

        def relay(i, p, peer):
            part = bias.at[p, :, pl.ds(i * (nzi // 2), nzi // 2)]
            remote(part, part, x_send.at[t], x_recv.at[t, 2 + i], peer).start()

        wait_for(raw.at[pl.ds(other, ROWS)], t_recv.at[t])

        def finish(i, c):
            x_s[i] = ln(raw[i].astype(F32), g_ref[...])
            return project(i, c)

        lax.fori_loop(other, other + ROWS, finish, 0)

        def block(step, c):
            @pl.when(step == 1)
            def _():
                wait_for(bias.at[up], x_recv.at[t, 0])
                relay(0, up, to_down)
                wait_for(bias.at[down], x_recv.at[t, 1])
                relay(1, down, to_up)

            @pl.when(step == 3)
            def _():
                for i in range(2):
                    wait_for(bias.at[far, :, pl.ds(i * (nzi // 2), nzi // 2)], x_recv.at[t, 2 + i])

            p = lax.rem(x + (step ^ (step >> 1)), nx)
            here = pl.ds(pl.multiple_of(p * quer, quer), quer)
            for r in range(TEAM):
                for k in range(per):
                    part = slice(k * CH, (k + 1) * CH)
                    s = score_s[r, p, part, :] + bias[p, k // nzi, k % nzi].astype(F32)
                    e_s[r, part, :] = jnp.exp2(s - jnp.max(s, axis=-1, keepdims=True)).astype(BF16)
                out = mm(e_s[r], v_s[r])
                top_s[r] = out[:, :width]
                low_s[r] = out[:, width:]
                top = top_s[r, pl.ds(0, quer, stride=HEADS), :]
                low = low_s[r, pl.ds(0, quer, stride=HEADS), :]
                for h in range(1, HEADS):
                    is_head = lane_head == h
                    rows = pl.ds(h, quer, stride=HEADS)
                    top = jnp.where(is_head, top_s[r, rows, :], top)
                    low = jnp.where(is_head, low_s[r, rows, :], low)
                hid = (gate_s[r, here, :] * (top / low)).astype(BF16)
                u = mm(hid, o_ref[...])
                if rounded:
                    u = u.astype(BF16).astype(F32)
                turn_s[pl.ds(r, quer, stride=TEAM), :] = res_s[r, here, :] + u
            stage[pl.ds(p * per, per)] = turn_s[...].astype(BF16).reshape(per, ROWS * TEAM, width)

            def send(k, c):
                m = p * per + lax.rem(mine + k, per)

                @pl.when(m != mine)
                def _():
                    remote(
                        stage.at[m], recv.at[mine], a_send.at[t], a_recv.at[t], member(m)
                    ).start()

                return c

            lax.fori_loop(0, per, send, 0)
            return c

        lax.fori_loop(0, nx, block, 0)
        recv[mine] = stage[mine]
        wait_for(recv.at[pl.ds(0, members - 1)], a_recv.at[t])

        wait_for(raw.at[pl.ds(own, ROWS)], t_send.at[t])
        if ny > 1:
            wait_for(bias.at[0, pl.ds(0, ny - 1), 0], y_send.at[t])
        wait_for(bias.at[0, :, pl.ds(0, nzi - 1)], z_send.at[t])
        wait_for(bias.at[pl.ds(0, 3)], x_send.at[t])
        wait_for(stage.at[pl.ds(0, members - 1)], a_send.at[t])

    def turned(recv, r):
        part = recv[...].astype(F32).reshape(members, ROWS, TEAM, width)[:, r]
        return part.reshape(members * TEAM, width).astype(BF16)

    for r in range(ROWS):
        raw0_s[own + r] = pair_ref[r]
    pl.semaphore_wait(barrier, members)
    update(0, sg_ref, sp_ref, sb_ref, so_ref, raw0_s, bias0_s, stage0_s, recv0_s, False)
    for r in range(ROWS):
        raw1_s[own + r] = turned(recv0_s, r)
    update(1, eg_ref, ep_ref, eb_ref, eo_ref, raw1_s, bias1_s, stage1_s, recv1_s, True)
    for r in range(ROWS):
        out_ref[r] = turned(recv1_s, r)


def solution(mesh):
    n = mesh.shape["row"]
    dims = (4, 4, 8) if n == 128 else (4, n // 16, 4)

    def body(pair, token_mask, sg, sp, sb, so, eg, ep, eb, eo):
        rows, count, width = pair.shape
        nx, ny, nz = dims
        per, members = ny * nz // 2, n // 2
        quer, span = per * ROWS, per * TEAM
        tall = quer * HEADS
        vmem = pl.BlockSpec(memory_space=pltpu.VMEM)
        dma = pltpu.SemaphoreType.DMA
        return pl.pallas_call(
            functools.partial(kernel, dims),
            out_shape=jax.ShapeDtypeStruct(pair.shape, BF16),
            in_specs=[vmem] * 10,
            out_specs=vmem,
            scratch_shapes=[
                pltpu.VMEM((TEAM, count, width), BF16),
                pltpu.VMEM((TEAM, count, width), BF16),
                pltpu.VMEM((TEAM, count, width), BF16),
                pltpu.VMEM((TEAM, count, 2 * width), BF16),
                pltpu.VMEM((TEAM, nx, tall, count), F32),
                pltpu.VMEM((TEAM, nx * quer, width), F32),
                pltpu.VMEM((TEAM, nx * quer, width), F32),
                pltpu.VMEM((TEAM, tall, count), BF16),
                pltpu.VMEM((TEAM, tall, width), F32),
                pltpu.VMEM((TEAM, tall, width), F32),
                pltpu.VMEM((quer * TEAM, width), F32),
                pltpu.VMEM((nx, ny, nz // 2, CH, count), BF16),
                pltpu.VMEM((nx, ny, nz // 2, CH, count), BF16),
                pltpu.VMEM((members, ROWS * TEAM, width), BF16),
                pltpu.VMEM((members, ROWS * TEAM, width), BF16),
                pltpu.VMEM((members, ROWS * TEAM, width), BF16),
                pltpu.VMEM((members, ROWS * TEAM, width), BF16),
                pltpu.VMEM((quer, span), BF16),
                pltpu.VMEM((tall, quer), BF16),
                pltpu.VMEM((width, 2 * width), BF16),
                pltpu.VMEM((width, 2 * width), BF16),
                dma((2,)), dma((2,)), dma((2,)), dma((2,)), dma((2,)), dma((2,)),
                dma((2,)), dma((2, 4)), dma((2,)), dma((2,)),
            ],
            compiler_params=pltpu.CompilerParams(
                collective_id=0, has_side_effects=True, vmem_limit_bytes=60 * 1024 * 1024
            ),
        )(
            pair, token_mask.reshape(1, count), sg.reshape(1, width), sp, sb.T, so,
            eg.reshape(1, width), ep, eb.T, eo,
        )

    return jax.shard_map(
        body,
        mesh=mesh,
        in_specs=(P(("rep", "row"), None, None), P("rep"), P(), P(), P(), P(), P(), P(), P(), P()),
        out_specs=P(("rep", "row"), None, None),
        check_vma=False,
    )
```

```python
import functools
import math

import jax
import jax.numpy as jnp
from jax import lax
from jax.experimental import pallas as pl
from jax.experimental.pallas import tpu as pltpu
from jax.sharding import PartitionSpec as P

MESH = pl.DeviceIdType.MESH
LOG2E = 1.4426950408889634
F32 = jnp.float32
BF16 = jnp.bfloat16
ROWS = 4
TEAM = 2 * ROWS
HEADS = 4
CH = ROWS * HEADS


def iota(shape, dim):
    return lax.broadcasted_iota(jnp.int32, shape, dim)


def one_hot(cond):
    return cond.astype(F32).astype(BF16)


def nt(a, b):
    return lax.dot_general(a, b, (((1,), (1,)), ((), ())), preferred_element_type=F32)


def mm(a, b):
    return jnp.dot(a, b, preferred_element_type=F32)


def ln(wide, gain):
    center = wide - jnp.mean(wide, axis=-1, keepdims=True)
    spread = jnp.mean(center * center, axis=-1, keepdims=True)
    return (center * lax.rsqrt(spread + 1e-05) * gain).astype(BF16)


def kernel(
    dims,
    pair_ref, mask_ref, sg_ref, sp_ref, sb_ref, so_ref, eg_ref, ep_ref, eb_ref, eo_ref,
    out_ref,
    raw0_s, raw1_s, x_s, v_s, score_s, gate_s, res_s, e_s, top_s, low_s, turn_s,
    bias0_s, bias1_s, stage0_s, stage1_s, recv0_s, recv1_s, pick_s, spread_s, wkv_s, wqg_s,
    t_send, t_recv, y_send, y_recv, z_send, z_recv, x_send, x_recv, a_send, a_recv,
):
    nx, ny, nz = dims
    nyi = ny // 2
    per = nyi * nz
    members = nx * per
    me = lax.axis_index("row")
    x, y, z = me // (ny * nz), (me // nz) % ny, me % nz
    cls, yi = y % 2, y // 2
    mine = (x * nyi + yi) * nz + z
    width = x_s.shape[2]
    count = x_s.shape[1]
    size = width // HEADS
    quer = per * ROWS
    tall = quer * HEADS
    span = per * TEAM
    group = nz * TEAM

    barrier = pltpu.get_barrier_semaphore()

    def greet_one(peer):
        pl.semaphore_signal(barrier, inc=1, device_id={"row": peer}, device_id_type=MESH)

    def member(m):
        return (2 * (m // nz) + cls) * nz + m % nz

    partner = me + nz * (1 - 2 * cls)
    greet_one(partner)

    def greet(s, c):
        greet_one(member(lax.rem(mine + s, members)))
        return c

    lax.fori_loop(1, members, greet, 0)

    def remote(src, dst, send, recv, peer):
        return pltpu.make_async_remote_copy(
            src_ref=src, dst_ref=dst, send_sem=send, recv_sem=recv,
            device_id={"row": peer}, device_id_type=MESH,
        )

    def wait_for(view, sem):
        pltpu.make_async_copy(view, view, sem).wait()

    def given(token):
        rest = token % group
        return token - rest + (rest // ROWS) % 2 * (nz * ROWS) + rest // TEAM * ROWS + rest % ROWS

    spread_s[...] = one_hot(iota((tall, quer), 0) // HEADS == iota((tall, quer), 1))
    lane_head = iota((quer, width), 1) // size
    head = (iota((tall, width), 0) % HEADS == iota((tall, width), 1) // size).astype(F32)
    far_mask = (1e9 * LOG2E)

    own = ROWS * cls
    other = ROWS - own
    up, down, far = lax.rem(x + 1, nx), lax.rem(x + nx - 1, nx), lax.rem(x + 2, nx)
    to_up = member(mine + (up - x) * per)
    to_down = member(mine + (down - x) * per)

    def half(ref, p, i):
        if nz > 1:
            return ref.at[p, :, pl.ds(i * (nz // 2), nz // 2)]
        return ref.at[p, pl.ds(i * (nyi // 2), nyi // 2)]

    def head_rows(b_ref, r):
        a, b = iota((CH, HEADS), 0), iota((CH, HEADS), 1)
        return mm(one_hot((a // HEADS == r) & (a % HEADS == b)), b_ref[...]).astype(BF16)

    def send_y(t, bias):
        def go(s, c):
            peer = member(mine + (lax.rem(yi + s, nyi) - yi) * nz)
            share = bias.at[x, yi, z]
            remote(share, share, y_send.at[t], y_recv.at[t], peer).start()
            return c

        lax.fori_loop(1, nyi, go, 0)

    def update(t, g_ref, p_ref, o_ref, raw, bias, stage, recv, on_last):
        row, col = iota((quer, span), 0), iota((quer, span), 1)
        token = row // ROWS * TEAM + ROWS * cls + row % ROWS
        pick_s[...] = one_hot((given(token) if t == 0 else token) == col)
        wkv_s[...] = p_ref[:, width : 3 * width]
        wqg_s[:, :width] = p_ref[:, :width]
        wqg_s[:, width:] = p_ref[:, 3 * width :]

        def project(i):
            pair = (i, i + 1)
            kv = [mm(x_s[k], wkv_s[...]) for k in pair]
            keys = [a[:, :width].astype(BF16) for a in kv]
            for k, a in zip(pair, kv):
                v_s[k, :, :width] = a[:, width:].astype(BF16)
            for p in range(nx):
                part = slice(p * span, (p + 1) * span)
                here = slice(p * quer, (p + 1) * quer)
                both = jnp.concatenate(
                    [x_s[i, part, :], x_s[i + 1, part, :], raw[i, part, :], raw[i + 1, part, :]],
                    axis=1,
                )
                both = mm(pick_s[...], both)
                normed = both[:, : 2 * width].astype(BF16)
                normed = jnp.concatenate([normed[:, :width], normed[:, width:]], axis=0)
                qg = mm(normed, wqg_s[...])
                gate = jax.nn.sigmoid(qg[:, width:].astype(BF16).astype(F32))
                q = (qg[:, :width] * (LOG2E / math.sqrt(size))).astype(BF16)
                q = mm(spread_s[...], jnp.concatenate([q[:quer], q[quer:]], axis=1))
                for n, k in enumerate(pair):
                    res_s[k, here, :] = both[:, (2 + n) * width : (3 + n) * width]
                    gate_s[k, here, :] = gate[n * quer : (n + 1) * quer]
                    one = (q[:, n * width : (n + 1) * width] * head).astype(BF16)
                    score_s[k, p] = nt(one, keys[n])

        project(own)
        if nyi > 1:
            wait_for(bias.at[0, pl.ds(0, nyi - 1), 0], y_recv.at[t])

        def send_z(s, c):
            peer = member(mine + lax.rem(z + s, nz) - z)
            line = bias.at[x, :, z]
            remote(line, line, z_send.at[t], z_recv.at[t], peer).start()
            return c

        if nz > 1:
            lax.fori_loop(1, nz, send_z, 0)
        project(own + 2)
        if nz > 1:
            wait_for(bias.at[0, :, pl.ds(0, nz - 1)], z_recv.at[t])

        for i in range(2):
            for sem, peer, h in ((0, to_down, i), (2, to_up, 1 - i)):
                part = half(bias, x, h)
                remote(part, part, x_send.at[t], x_recv.at[t, sem + h], peer).start()

        wait_for(raw.at[pl.ds(other, ROWS)], t_recv.at[t])
        for r in range(2):
            x_s[other + r] = ln(raw[other + r].astype(F32), g_ref[...])
        project(other)

        wait_for(half(bias, up, 0), x_recv.at[t, 0])
        part = half(bias, up, 0)
        remote(part, part, x_send.at[t], x_recv.at[t, 4], to_down).start()
        wait_for(half(bias, down, 1), x_recv.at[t, 3])
        part = half(bias, down, 1)
        remote(part, part, x_send.at[t], x_recv.at[t, 5], to_up).start()

        for r in range(2, ROWS):
            x_s[other + r] = ln(raw[other + r].astype(F32), g_ref[...])
        project(other + 2)

        def block(step, c):
            @pl.when(step == 1)
            def _():
                wait_for(half(bias, up, 1), x_recv.at[t, 1])

            @pl.when(step == 2)
            def _():
                wait_for(half(bias, down, 0), x_recv.at[t, 2])

            @pl.when(step == 3)
            def _():
                on_last()
                wait_for(half(bias, far, 0), x_recv.at[t, 4])
                wait_for(half(bias, far, 1), x_recv.at[t, 5])

            p = lax.rem(x + (step ^ (step >> 1)), nx)
            here = pl.ds(pl.multiple_of(p * quer, quer), quer)
            for r in range(TEAM):
                for k in range(per):
                    part = slice(k * CH, (k + 1) * CH)
                    s = score_s[r, p, part, :] + bias[p, k // nz, k % nz].astype(F32)
                    e_s[r, part, :] = jnp.exp2(s - jnp.max(s, axis=-1, keepdims=True)).astype(BF16)
                out = mm(e_s[r], v_s[r])
                top_s[r] = out[:, :width]
                low_s[r] = out[:, width:]
            hid = []
            for r in range(TEAM):
                top = top_s[r, pl.ds(0, quer, stride=HEADS), :]
                low = low_s[r, pl.ds(0, quer, stride=HEADS), :]
                for h in range(1, HEADS):
                    rows = pl.ds(h, quer, stride=HEADS)
                    top = jnp.where(lane_head == h, top_s[r, rows, :], top)
                    low = jnp.where(lane_head == h, low_s[r, rows, :], low)
                hid.append((gate_s[r, here, :] * (top / low)).astype(BF16))
            u = mm(jnp.concatenate(hid, axis=0), o_ref[...])
            if t == 1:
                u = u.astype(BF16).astype(F32)
            for r in range(TEAM):
                turn_s[pl.ds(r, quer, stride=TEAM), :] = (
                    res_s[r, here, :] + u[r * quer : (r + 1) * quer]
                )
            stage[pl.ds(p * per, per)] = turn_s[...].astype(BF16).reshape(per, ROWS * TEAM, width)

            def send(k, c):
                m = p * per + lax.rem(mine + k, per)

                @pl.when(m != mine)
                def _():
                    remote(
                        stage.at[m], recv.at[mine], a_send.at[t], a_recv.at[t, step], member(m)
                    ).start()

                return c

            lax.fori_loop(0, per, send, 0)

            @pl.when(step == 0)
            def _():
                recv[mine] = stage[mine]

            return c

        lax.fori_loop(0, nx, block, 0)

    def taken(t, recv, n):
        p = (x, down, up, far)[n]
        wait_for(recv.at[pl.ds(0, per - (n == 0))], a_recv.at[t, n])
        part = recv[pl.ds(p * per, per)].astype(F32)
        return p, part.reshape(per, ROWS, TEAM, width)

    def arrive(n):
        p, part = taken(0, recv0_s, n)
        here = pl.ds(pl.multiple_of(p * span, span), span)
        total = None
        for r in range(ROWS):
            row = part[:, r].reshape(span, width)
            raw1_s[own + r, here, :] = row.astype(BF16)
            normed = ln(row, eg_ref[...])
            x_s[own + r, here, :] = normed
            term = nt(head_rows(eb_ref, r), normed)
            total = term if total is None else total + term
        piece = raw1_s.at[pl.ds(own, ROWS), here, :]
        remote(piece, piece, t_send.at[1], t_recv.at[1], partner).start()
        order = given(p * span + iota((count, span), 1))
        order = one_hot(iota((count, span), 0) == order)
        mask = mm(jnp.broadcast_to(mask_ref[...].astype(F32).astype(BF16), (CH, count)), order)
        bias1_s[x, yi, z, :, here] = (total * LOG2E + (mask - 1.0) * far_mask).astype(BF16)

    def drain(t, raw, bias, stage):
        wait_for(raw.at[pl.ds(own, ROWS)], t_send.at[t])
        if nyi > 1:
            wait_for(bias.at[0, pl.ds(0, nyi - 1), 0], y_send.at[t])
        if nz > 1:
            wait_for(bias.at[0, :, pl.ds(0, nz - 1)], z_send.at[t])
        wait_for(bias.at[pl.ds(0, 3)], x_send.at[t])
        wait_for(stage.at[pl.ds(0, members - 1)], a_send.at[t])

    for r in range(ROWS):
        raw0_s[own + r] = pair_ref[r]
    v_s[:, :, width:] = jnp.ones((TEAM, count, width), BF16)
    total = None
    for r in range(ROWS):
        normed = ln(pair_ref[r].astype(F32), sg_ref[...])
        x_s[own + r] = normed
        term = nt(head_rows(sb_ref, r), normed)
        total = term if total is None else total + term
    mask = mask_ref[...].astype(F32)
    bias0_s[x, yi, z] = (total * LOG2E + (mask - 1.0) * far_mask).astype(BF16)
    pl.semaphore_wait(barrier, members)
    send_y(0, bias0_s)
    rows = raw0_s.at[pl.ds(own, ROWS)]
    remote(rows, rows, t_send.at[0], t_recv.at[0], partner).start()

    def early():
        arrive(0)
        arrive(1)

    update(0, sg_ref, sp_ref, so_ref, raw0_s, bias0_s, stage0_s, recv0_s, early)
    arrive(2)
    arrive(3)
    send_y(1, bias1_s)
    update(1, eg_ref, ep_ref, eo_ref, raw1_s, bias1_s, stage1_s, recv1_s, lambda: None)
    order = one_hot(iota((span, span), 0) == given(iota((span, span), 1)))
    for n in range(nx):
        p, part = taken(1, recv1_s, n)
        here = pl.ds(pl.multiple_of(p * span, span), span)
        part = jnp.concatenate([part[:, r].reshape(span, width) for r in range(ROWS)], axis=1)
        part = mm(order, part.astype(BF16)).astype(BF16)
        for r in range(ROWS):
            out_ref[r, here, :] = part[:, r * width : (r + 1) * width]
    drain(0, raw0_s, bias0_s, stage0_s)
    drain(1, raw1_s, bias1_s, stage1_s)


def solution(mesh):
    n = mesh.shape["row"]
    dims = (4, 4, 8) if n == 128 else (4, 4, 1) if n == 16 else (4, 2, 2)

    def body(pair, token_mask, sg, sp, sb, so, eg, ep, eb, eo):
        rows, count, width = pair.shape
        nx, ny, nz = dims
        per, members = ny * nz // 2, n // 2
        quer, span = per * ROWS, per * TEAM
        tall = quer * HEADS
        vmem = pl.BlockSpec(memory_space=pltpu.VMEM)
        dma = pltpu.SemaphoreType.DMA
        return pl.pallas_call(
            functools.partial(kernel, dims),
            out_shape=jax.ShapeDtypeStruct(pair.shape, BF16),
            in_specs=[vmem] * 10,
            out_specs=vmem,
            scratch_shapes=[
                pltpu.VMEM((TEAM, count, width), BF16),
                pltpu.VMEM((TEAM, count, width), BF16),
                pltpu.VMEM((TEAM, count, width), BF16),
                pltpu.VMEM((TEAM, count, 2 * width), BF16),
                pltpu.VMEM((TEAM, nx, tall, count), F32),
                pltpu.VMEM((TEAM, nx * quer, width), F32),
                pltpu.VMEM((TEAM, nx * quer, width), F32),
                pltpu.VMEM((TEAM, tall, count), BF16),
                pltpu.VMEM((TEAM, tall, width), F32),
                pltpu.VMEM((TEAM, tall, width), F32),
                pltpu.VMEM((quer * TEAM, width), F32),
                pltpu.VMEM((nx, ny // 2, nz, CH, count), BF16),
                pltpu.VMEM((nx, ny // 2, nz, CH, count), BF16),
                pltpu.VMEM((members, ROWS * TEAM, width), BF16),
                pltpu.VMEM((members, ROWS * TEAM, width), BF16),
                pltpu.VMEM((members, ROWS * TEAM, width), BF16),
                pltpu.VMEM((members, ROWS * TEAM, width), BF16),
                pltpu.VMEM((quer, span), BF16),
                pltpu.VMEM((tall, quer), BF16),
                pltpu.VMEM((width, 2 * width), BF16),
                pltpu.VMEM((width, 2 * width), BF16),
                dma((2,)), dma((2,)), dma((2,)), dma((2,)), dma((2,)), dma((2,)),
                dma((2,)), dma((2, 6)), dma((2,)), dma((2, 4)),
            ],
            compiler_params=pltpu.CompilerParams(
                collective_id=0, has_side_effects=True, vmem_limit_bytes=60 * 1024 * 1024
            ),
        )(
            pair, token_mask.reshape(1, count), sg.reshape(1, width), sp, sb.T, so,
            eg.reshape(1, width), ep, eb.T, eo,
        )

    return jax.shard_map(
        body,
        mesh=mesh,
        in_specs=(P(("rep", "row"), None, None), P("rep"), P(), P(), P(), P(), P(), P(), P(), P()),
        out_specs=P(("rep", "row"), None, None),
        check_vma=False,
    )
```

```python
import functools
import math

import jax
import jax.numpy as jnp
from jax import lax
from jax.experimental import pallas as pl
from jax.experimental.pallas import tpu as pltpu
from jax.sharding import PartitionSpec as P

MESH = pl.DeviceIdType.MESH
LOG2E = 1.4426950408889634
F32 = jnp.float32
BF16 = jnp.bfloat16
ROWS = 4
TEAM = 2 * ROWS
HEADS = 4
CH = ROWS * HEADS


def iota(shape, dim):
    return lax.broadcasted_iota(jnp.int32, shape, dim)


def one_hot(cond):
    return cond.astype(F32).astype(BF16)


def nt(a, b):
    return lax.dot_general(a, b, (((1,), (1,)), ((), ())), preferred_element_type=F32)


def mm(a, b):
    return jnp.dot(a, b, preferred_element_type=F32)


def ln(wide, gain):
    center = wide - jnp.mean(wide, axis=-1, keepdims=True)
    spread = jnp.mean(center * center, axis=-1, keepdims=True)
    return (center * lax.rsqrt(spread + 1e-05) * gain).astype(BF16)


def kernel(
    dims,
    pair_ref, mask_ref, sg_ref, sp_ref, sb_ref, so_ref, eg_ref, ep_ref, eb_ref, eo_ref,
    out_ref,
    raw0_s, raw1_s, x_s, v_s, score_s, gate_s, res_s, e_s, top_s, low_s, turn_s,
    bias0_s, bias1_s, stage0_s, stage1_s, recv0_s, recv1_s, pick_s, spread_s, wkv_s, wqg_s,
    t_send, t_recv, z_send, z_recv, x_send, x_recv, a_send, a_recv,
):
    nx, ny, nz = dims
    nyi, nzh = ny // 2, nz // 2
    near = nyi * nzh
    per = 2 * near
    members = nx * per
    me = lax.axis_index("row")
    x, y, z = me // (ny * nz), (me // nz) % ny, me % nz
    cls, yi = y % 2, y // 2
    hz, local = z // nzh, yi * nzh + z % nzh
    mine = (x * nyi + yi) * nz + z
    width = x_s.shape[2]
    count = x_s.shape[1]
    size = width // HEADS
    quer = near * ROWS
    tall = quer * HEADS
    span = per * TEAM
    group = nz * TEAM

    barrier = pltpu.get_barrier_semaphore()

    def greet_one(peer):
        pl.semaphore_signal(barrier, inc=1, device_id={"row": peer}, device_id_type=MESH)

    def member(m):
        return (2 * (m // nz) + cls) * nz + m % nz

    def place(p, half, i):
        return (p * nyi + i // nzh) * nz + half * nzh + i % nzh

    partner = me + nz * (1 - 2 * cls)
    greet_one(partner)

    def greet(s, c):
        greet_one(member(lax.rem(mine + s, members)))
        return c

    lax.fori_loop(1, members, greet, 0)

    def remote(src, dst, send, recv, peer):
        return pltpu.make_async_remote_copy(
            src_ref=src, dst_ref=dst, send_sem=send, recv_sem=recv,
            device_id={"row": peer}, device_id_type=MESH,
        )

    def wait_for(view, sem):
        pltpu.make_async_copy(view, view, sem).wait()

    def given(token):
        rest = token % group
        return token - rest + (rest // ROWS) % 2 * (nz * ROWS) + rest // TEAM * ROWS + rest % ROWS

    spread_s[...] = one_hot(iota((tall, quer), 0) // HEADS == iota((tall, quer), 1))
    lane_head = iota((quer, width), 1) // size
    head = (iota((tall, width), 0) % HEADS == iota((tall, width), 1) // size).astype(F32)
    far_mask = 1e9 * LOG2E

    own = ROWS * cls
    other = ROWS - own
    up, down, far = lax.rem(x + 1, nx), lax.rem(x + nx - 1, nx), lax.rem(x + 2, nx)
    to_up = member(mine + (up - x) * per)
    to_down = member(mine + (down - x) * per)

    def part_of(bias, p, late):
        half = (hz + late) % 2
        return bias.at[p, :, pl.ds(half * nzh, nzh)]

    def quarter(bias, p, i, late):
        half = (hz + late) % 2
        return bias.at[p, i, pl.ds(half * nzh, nzh)]

    def head_rows(b_ref, r):
        a, b = iota((CH, HEADS), 0), iota((CH, HEADS), 1)
        return mm(one_hot((a // HEADS == r) & (a % HEADS == b)), b_ref[...]).astype(BF16)

    def gather_plane(t, bias):
        for late in range(2):

            def go(s, c):
                peer = member(place(x, (hz + late) % 2, lax.rem(local + s, near)))
                share = bias.at[x, yi, z]
                remote(share, share, z_send.at[t], z_recv.at[t, late], peer).start()
                return c

            lax.fori_loop(1 - late, near, go, 0)

    def to_neighbours(t, bias, late):
        part = part_of(bias, x, late)
        remote(part, part, x_send.at[t], x_recv.at[t, late], to_down).start()
        remote(part, part, x_send.at[t], x_recv.at[t, 2 + late], to_up).start()

    def relay(t, bias, late):
        wait_for(part_of(bias, up, late), x_recv.at[t, late])
        part = quarter(bias, up, 0, late)
        remote(part, part, x_send.at[t], x_recv.at[t, 4 + late], to_down).start()
        wait_for(part_of(bias, down, late), x_recv.at[t, 2 + late])
        part = quarter(bias, down, 1, late)
        remote(part, part, x_send.at[t], x_recv.at[t, 6 + late], to_up).start()

    def from_far(t, bias, late):
        wait_for(quarter(bias, far, 0, late), x_recv.at[t, 4 + late])
        wait_for(quarter(bias, far, 1, late), x_recv.at[t, 6 + late])

    def update(t, g_ref, p_ref, o_ref, raw, bias, stage, recv, on_last):
        row, col = iota((2 * quer, span), 0), iota((2 * quer, span), 1)
        share = row // ROWS
        token = place(0, share // near, share % near) * TEAM + ROWS * cls + row % ROWS
        pick_s[...] = one_hot((given(token) if t == 0 else token) == col)
        wkv_s[...] = p_ref[:, width : 3 * width]
        wqg_s[:, :width] = p_ref[:, :width]
        wqg_s[:, width:] = p_ref[:, 3 * width :]

        def project(i):
            pair = (i, i + 1)
            kv = [mm(x_s[k], wkv_s[...]) for k in pair]
            keys = [a[:, :width].astype(BF16) for a in kv]
            for k, a in zip(pair, kv):
                v_s[k, :, :width] = a[:, width:].astype(BF16)
            for p in range(nx):
                part = slice(p * span, (p + 1) * span)
                both = jnp.concatenate(
                    [x_s[i, part, :], x_s[i + 1, part, :], raw[i, part, :], raw[i + 1, part, :]],
                    axis=1,
                )
                both = mm(pick_s[...], both)
                normed = both[:, : 2 * width].astype(BF16)
                normed = jnp.concatenate([normed[:, :width], normed[:, width:]], axis=0)
                qg = mm(normed, wqg_s[...])
                gate = jax.nn.sigmoid(qg[:, width:].astype(BF16).astype(F32))
                q = (qg[:, :width] * (LOG2E / math.sqrt(size))).astype(BF16)
                for n, k in enumerate(pair):
                    res_s[k, p] = both[:, (2 + n) * width : (3 + n) * width]
                    gate_s[k, p] = gate[2 * n * quer : 2 * (n + 1) * quer]
                for half in range(2):
                    lo = half * quer
                    two = [q[lo + 2 * n * quer : lo + (2 * n + 1) * quer] for n in range(2)]
                    wide = mm(spread_s[...], jnp.concatenate(two, axis=1))
                    for n, k in enumerate(pair):
                        one = (wide[:, n * width : (n + 1) * width] * head).astype(BF16)
                        score_s[k, p, half] = nt(one, keys[n])

        def finish(i):
            for k in (i, i + 1):
                x_s[k] = ln(raw[k].astype(F32), g_ref[...])
            project(i)

        project(own)
        project(own + 2)
        wait_for(bias.at[0, 0, pl.ds(0, near - 1)], z_recv.at[t, 0])
        to_neighbours(t, bias, 0)
        if t == 0:
            wait_for(raw.at[pl.ds(other, 2)], t_recv.at[0])
        else:
            wait_for(raw.at[pl.ds(other, ROWS)], t_recv.at[2])
        finish(other)
        wait_for(part_of(bias, 0, 0), z_recv.at[t, 1])
        to_neighbours(t, bias, 1)

        def unit(n, c):
            @pl.when(n == 2)
            def _():
                relay(t, bias, 0)

            @pl.when(n == 4)
            def _():
                if t == 0:
                    wait_for(raw.at[pl.ds(other + 2, 2)], t_recv.at[1])
                finish(other + 2)
                relay(t, bias, 1)

            @pl.when(n == 8)
            def _():
                from_far(t, bias, 0)

            @pl.when(n == 14)
            def _():
                on_last()
                from_far(t, bias, 1)

            q = (n - 8) // 2
            rel = jnp.where(n >= 8, jnp.where((q == 0) | (q == 3), 3, q), jnp.maximum(n % 4 - 1, 0))
            late = jnp.where(n >= 8, (q > 0).astype(jnp.int32), (n % 4 == 1).astype(jnp.int32))
            kind = jnp.where(n >= 8, n % 2, n // 4)
            p = lax.rem(x + (rel ^ (rel >> 1)), nx)
            half = (hz + late) % 2
            side = (cls + kind) % 2
            base = ROWS * side
            for r in range(ROWS):
                for k in range(near):
                    part = slice(k * CH, (k + 1) * CH)
                    add = bias[p, k // nzh, half * nzh + k % nzh].astype(F32)
                    s = score_s[base + r, p, half, part, :] + add
                    e_s[r, part, :] = jnp.exp2(s - jnp.max(s, axis=-1, keepdims=True)).astype(BF16)
                out = mm(e_s[r], v_s[base + r])
                top_s[r] = out[:, :width]
                low_s[r] = out[:, width:]
            here = pl.ds(pl.multiple_of(half * quer, quer), quer)
            hid = []
            for r in range(ROWS):
                top = top_s[r, pl.ds(0, quer, stride=HEADS), :]
                low = low_s[r, pl.ds(0, quer, stride=HEADS), :]
                for h in range(1, HEADS):
                    rows = pl.ds(h, quer, stride=HEADS)
                    top = jnp.where(lane_head == h, top_s[r, rows, :], top)
                    low = jnp.where(lane_head == h, low_s[r, rows, :], low)
                hid.append((gate_s[base + r, p, here, :] * (top / low)).astype(BF16))
            u = mm(jnp.concatenate(hid, axis=0), o_ref[...])
            if t == 1:
                u = u.astype(BF16).astype(F32)
            for r in range(ROWS):
                turn_s[pl.ds(r, quer, stride=ROWS), :] = (
                    res_s[base + r, p, here, :] + u[r * quer : (r + 1) * quer]
                )
            turned = turn_s[...].astype(BF16).reshape(near, CH, width)
            for i in range(nyi):
                stage[pl.ds(place(p, half, i * nzh), nzh), side] = turned[i * nzh : (i + 1) * nzh]

            def send(k, c):
                m = place(p, half, lax.rem(local + k, near))

                @pl.when(m != mine)
                def _():
                    remote(
                        stage.at[m, side], recv.at[mine, side], a_send.at[t], a_recv.at[t, rel],
                        member(m),
                    ).start()

                return c

            lax.fori_loop(0, near, send, 0)

            @pl.when((n == 0) | (n == 4))
            def _():
                recv[mine, side] = stage[mine, side]

            return c

        lax.fori_loop(0, 16, unit, 0)

    def taken(t, recv, n):
        p = (x, down, up, far)[n]
        wait_for(recv.at[pl.ds(0, per - (n == 0))], a_recv.at[t, n])
        return p, recv[pl.ds(p * per, per)].reshape(per * 2 * CH, width)

    def in_lanes(part, pieces):
        rows = part.shape[0] // pieces
        return jnp.concatenate([part[i * rows : (i + 1) * rows] for i in range(pieces)], axis=1)

    def arrive(n):
        p, part = taken(0, recv0_s, n)
        here = pl.ds(pl.multiple_of(p * span, span), span)
        four = 4 * 2 * CH
        rows = four // ROWS
        o, i = iota((four, four), 0), iota((four, four), 1)
        order = (o % rows) // ROWS * CH + o // rows * ROWS + o % ROWS
        part = mm(one_hot(order == i), in_lanes(part, per // 4))
        total = None
        for r in range(ROWS):
            row = jnp.concatenate(
                [
                    part[r * rows : (r + 1) * rows, k * width : (k + 1) * width]
                    for k in range(per // 4)
                ],
                axis=0,
            )
            raw1_s[own + r, here, :] = row.astype(BF16)
            normed = ln(row, eg_ref[...])
            x_s[own + r, here, :] = normed
            term = nt(head_rows(eb_ref, r), normed)
            total = term if total is None else total + term
        piece = raw1_s.at[pl.ds(own, ROWS), here, :]
        remote(piece, piece, t_send.at[1], t_recv.at[2], partner).start()
        order = given(p * span + iota((count, span), 1))
        order = one_hot(iota((count, span), 0) == order)
        mask = mm(jnp.broadcast_to(mask_ref[...].astype(F32).astype(BF16), (CH, count)), order)
        bias1_s[x, yi, z, :, here] = (total * LOG2E + (mask - 1.0) * far_mask).astype(BF16)

    def drain(t, raw, bias, stage):
        wait_for(raw.at[pl.ds(own, ROWS)], t_send.at[t])
        wait_for(bias.at[0, 0, pl.ds(0, near - 1)], z_send.at[t])
        wait_for(part_of(bias, 0, 0), z_send.at[t])
        wait_for(bias.at[pl.ds(0, 3)], x_send.at[t])
        wait_for(stage.at[pl.ds(0, members - 1)], a_send.at[t])

    for r in range(ROWS):
        raw0_s[own + r] = pair_ref[r]
    v_s[:, :, width:] = jnp.ones((TEAM, count, width), BF16)
    total = None
    for r in range(ROWS):
        normed = ln(pair_ref[r].astype(F32), sg_ref[...])
        x_s[own + r] = normed
        term = nt(head_rows(sb_ref, r), normed)
        total = term if total is None else total + term
    mask = mask_ref[...].astype(F32)
    bias0_s[x, yi, z] = (total * LOG2E + (mask - 1.0) * far_mask).astype(BF16)
    pl.semaphore_wait(barrier, members)
    gather_plane(0, bias0_s)
    for i in range(2):
        rows = raw0_s.at[pl.ds(own + 2 * i, 2)]
        remote(rows, rows, t_send.at[0], t_recv.at[i], partner).start()

    update(0, sg_ref, sp_ref, so_ref, raw0_s, bias0_s, stage0_s, recv0_s, lambda: arrive(0))
    arrive(1)
    arrive(2)
    arrive(3)
    gather_plane(1, bias1_s)
    update(1, eg_ref, ep_ref, eo_ref, raw1_s, bias1_s, stage1_s, recv1_s, lambda: None)
    line = nz * 2 * CH
    rows = line // ROWS
    o, i = iota((line, line), 0), iota((line, line), 1)
    order = (o % rows) // ROWS
    order = ((order % nz) * 2 + order // nz) * CH + o // rows * ROWS + o % ROWS
    order = one_hot(order == i)
    for n in range(nx):
        p, part = taken(1, recv1_s, n)
        part = mm(order, in_lanes(part, nyi)).astype(BF16)
        for k in range(nyi):
            here = pl.ds(pl.multiple_of(p * span + k * group, group), group)
            for r in range(ROWS):
                out_ref[r, here, :] = part[
                    r * rows : (r + 1) * rows, k * width : (k + 1) * width
                ]
    drain(0, raw0_s, bias0_s, stage0_s)
    drain(1, raw1_s, bias1_s, stage1_s)


def solution(mesh):
    n = mesh.shape["row"]
    dims = (4, 4, n // 16)

    def body(pair, token_mask, sg, sp, sb, so, eg, ep, eb, eo):
        rows, count, width = pair.shape
        nx, ny, nz = dims
        near, members = ny // 2 * (nz // 2), n // 2
        quer, span = near * ROWS, 2 * near * TEAM
        tall = quer * HEADS
        vmem = pl.BlockSpec(memory_space=pltpu.VMEM)
        dma = pltpu.SemaphoreType.DMA
        return pl.pallas_call(
            functools.partial(kernel, dims),
            out_shape=jax.ShapeDtypeStruct(pair.shape, BF16),
            in_specs=[vmem] * 10,
            out_specs=vmem,
            scratch_shapes=[
                pltpu.VMEM((TEAM, count, width), BF16),
                pltpu.VMEM((TEAM, count, width), BF16),
                pltpu.VMEM((TEAM, count, width), BF16),
                pltpu.VMEM((TEAM, count, 2 * width), BF16),
                pltpu.VMEM((TEAM, nx, 2, tall, count), F32),
                pltpu.VMEM((TEAM, nx, 2 * quer, width), F32),
                pltpu.VMEM((TEAM, nx, 2 * quer, width), F32),
                pltpu.VMEM((ROWS, tall, count), BF16),
                pltpu.VMEM((ROWS, tall, width), F32),
                pltpu.VMEM((ROWS, tall, width), F32),
                pltpu.VMEM((quer * ROWS, width), F32),
                pltpu.VMEM((nx, ny // 2, nz, CH, count), BF16),
                pltpu.VMEM((nx, ny // 2, nz, CH, count), BF16),
                pltpu.VMEM((members, 2, CH, width), BF16),
                pltpu.VMEM((members, 2, CH, width), BF16),
                pltpu.VMEM((members, 2, CH, width), BF16),
                pltpu.VMEM((members, 2, CH, width), BF16),
                pltpu.VMEM((2 * quer, span), BF16),
                pltpu.VMEM((tall, quer), BF16),
                pltpu.VMEM((width, 2 * width), BF16),
                pltpu.VMEM((width, 2 * width), BF16),
                dma((2,)), dma((3,)), dma((2,)), dma((2, 2)),
                dma((2,)), dma((2, 8)), dma((2,)), dma((2, 4)),
            ],
            compiler_params=pltpu.CompilerParams(
                collective_id=0, has_side_effects=True, vmem_limit_bytes=60 * 1024 * 1024
            ),
        )(
            pair, token_mask.reshape(1, count), sg.reshape(1, width), sp, sb.T, so,
            eg.reshape(1, width), ep, eb.T, eo,
        )

    return jax.shard_map(
        body,
        mesh=mesh,
        in_specs=(P(("rep", "row"), None, None), P("rep"), P(), P(), P(), P(), P(), P(), P(), P()),
        out_specs=P(("rep", "row"), None, None),
        check_vma=False,
    )
```

```python
import functools
import math

import jax
import jax.numpy as jnp
from jax import lax
from jax.experimental import pallas as pl
from jax.experimental.pallas import tpu as pltpu
from jax.sharding import PartitionSpec as P

MESH = pl.DeviceIdType.MESH
LOG2E = 1.4426950408889634
F32 = jnp.float32
BF16 = jnp.bfloat16
ROWS = 4
TEAM = 2 * ROWS
HEADS = 4
CH = ROWS * HEADS


def iota(shape, dim):
    return lax.broadcasted_iota(jnp.int32, shape, dim)


def one_hot(cond):
    return cond.astype(F32).astype(BF16)


def nt(a, b):
    return lax.dot_general(a, b, (((1,), (1,)), ((), ())), preferred_element_type=F32)


def mm(a, b):
    return jnp.dot(a, b, preferred_element_type=F32)


def ln(wide, gain):
    center = wide - jnp.mean(wide, axis=-1, keepdims=True)
    spread = jnp.mean(center * center, axis=-1, keepdims=True)
    return (center * lax.rsqrt(spread + 1e-05) * gain).astype(BF16)


def kernel(
    dims,
    pair_ref, mask_ref, sg_ref, sp_ref, sb_ref, so_ref, eg_ref, ep_ref, eb_ref, eo_ref,
    out_ref,
    raw0_s, raw1_s, x_s, v_s, score_s, gate_s, res_s, e_s, top_s, low_s, turn_s,
    bias0_s, bias1_s, stage0_s, stage1_s, recv0_s, recv1_s, pick_s, spread_s, wkv_s, wqg_s, q_s,
    t_send, t_recv, z_send, z_recv, x_send, x_recv, a_send, a_recv,
):
    nx, ny, nz = dims
    nyi, nzh = ny // 2, nz // 2
    near = nyi * nzh
    per = 2 * near
    members = nx * per
    me = lax.axis_index("row")
    x, y, z = me // (ny * nz), (me // nz) % ny, me % nz
    cls, yi = y % 2, y // 2
    hz, local = z // nzh, yi * nzh + z % nzh
    mine = (x * nyi + yi) * nz + z
    width = x_s.shape[2]
    count = x_s.shape[1]
    size = width // HEADS
    quer = per * ROWS
    tall = quer * HEADS
    span = per * TEAM
    group = nz * TEAM

    barrier = pltpu.get_barrier_semaphore()

    def greet_one(peer):
        pl.semaphore_signal(barrier, inc=1, device_id={"row": peer}, device_id_type=MESH)

    def member(m):
        return (2 * (m // nz) + cls) * nz + m % nz

    def place(p, half, i):
        return (p * nyi + i // nzh) * nz + half * nzh + i % nzh

    partner = me + nz * (1 - 2 * cls)
    greet_one(partner)

    def greet(s, c):
        greet_one(member(lax.rem(mine + s, members)))
        return c

    lax.fori_loop(1, members, greet, 0)

    def remote(src, dst, send, recv, peer):
        return pltpu.make_async_remote_copy(
            src_ref=src, dst_ref=dst, send_sem=send, recv_sem=recv,
            device_id={"row": peer}, device_id_type=MESH,
        )

    def wait_for(view, sem):
        pltpu.make_async_copy(view, view, sem).wait()

    def given(token):
        rest = token % group
        return token - rest + (rest // ROWS) % 2 * (nz * ROWS) + rest // TEAM * ROWS + rest % ROWS

    spread_s[...] = one_hot(iota((tall, quer), 0) // HEADS == iota((tall, quer), 1))
    lane_head = iota((quer, width), 1) // size
    head = (iota((tall, width), 0) % HEADS == iota((tall, width), 1) // size).astype(F32)
    far_mask = 1e9 * LOG2E

    own = ROWS * cls
    other = ROWS - own
    up, down, far = lax.rem(x + 1, nx), lax.rem(x + nx - 1, nx), lax.rem(x + 2, nx)
    to_up = member(mine + (up - x) * per)
    to_down = member(mine + (down - x) * per)

    def part_of(bias, p, late):
        half = (hz + late) % 2
        return bias.at[p, :, pl.ds(half * nzh, nzh)]

    def quarter(bias, p, i, late):
        half = (hz + late) % 2
        return bias.at[p, i, pl.ds(half * nzh, nzh)]

    def head_rows(b_ref, r):
        a, b = iota((CH, HEADS), 0), iota((CH, HEADS), 1)
        return mm(one_hot((a // HEADS == r) & (a % HEADS == b)), b_ref[...]).astype(BF16)

    def gather_plane(t, bias):
        for late in range(2):

            def go(s, c):
                peer = member(place(x, (hz + late) % 2, lax.rem(local + s, near)))
                share = bias.at[x, yi, z]
                remote(share, share, z_send.at[t], z_recv.at[t, late], peer).start()
                return c

            lax.fori_loop(1 - late, near, go, 0)

    def to_neighbours(t, bias, late):
        part = part_of(bias, x, late)
        remote(part, part, x_send.at[t], x_recv.at[t, late], to_down).start()
        remote(part, part, x_send.at[t], x_recv.at[t, 2 + late], to_up).start()

    def relay(t, bias, late):
        wait_for(part_of(bias, up, late), x_recv.at[t, late])
        part = quarter(bias, up, 0, late)
        remote(part, part, x_send.at[t], x_recv.at[t, 4 + late], to_down).start()
        wait_for(part_of(bias, down, late), x_recv.at[t, 2 + late])
        part = quarter(bias, down, 1, late)
        remote(part, part, x_send.at[t], x_recv.at[t, 6 + late], to_up).start()

    def from_far(t, bias, late):
        wait_for(quarter(bias, far, 0, late), x_recv.at[t, 4 + late])
        wait_for(quarter(bias, far, 1, late), x_recv.at[t, 6 + late])

    def update(t, g_ref, p_ref, o_ref, raw, bias, stage, recv):
        row, col = iota((quer, span), 0), iota((quer, span), 1)
        token = row // ROWS * TEAM + ROWS * cls + row % ROWS
        pick_s[...] = one_hot((given(token) if t == 0 else token) == col)
        wkv_s[...] = p_ref[:, width : 3 * width]
        wqg_s[:, :width] = p_ref[:, :width]
        wqg_s[:, width:] = p_ref[:, 3 * width :]

        def project(i):
            pair = (i, i + 1)
            kv = [mm(x_s[k], wkv_s[...]) for k in pair]
            keys = [a[:, :width].astype(BF16) for a in kv]
            for k, a in zip(pair, kv):
                v_s[k, :, :width] = a[:, width:].astype(BF16)
            for p in range(nx):
                part = slice(p * span, (p + 1) * span)
                both = jnp.concatenate(
                    [x_s[i, part, :], x_s[i + 1, part, :], raw[i, part, :], raw[i + 1, part, :]],
                    axis=1,
                )
                both = mm(pick_s[...], both)
                normed = both[:, : 2 * width].astype(BF16)
                normed = jnp.concatenate([normed[:, :width], normed[:, width:]], axis=0)
                qg = mm(normed, wqg_s[...])
                gate = jax.nn.sigmoid(qg[:, width:].astype(BF16).astype(F32))
                q = (qg[:, :width] * (LOG2E / math.sqrt(size))).astype(BF16)
                q = mm(spread_s[...], jnp.concatenate([q[:quer], q[quer:]], axis=1))
                for n, k in enumerate(pair):
                    res_s[k, p] = both[:, (2 + n) * width : (3 + n) * width]
                    gate_s[k, p] = gate[n * quer : (n + 1) * quer]
                    one = q[:, n * width : (n + 1) * width] * head
                    q_s[n, p * tall : (p + 1) * tall, :] = one.astype(BF16)
            for n, k in enumerate(pair):
                score_s[k] = nt(q_s[n], keys[n]).reshape(nx, tall, count)

        def finish(i):
            for k in (i, i + 1):
                x_s[k] = ln(raw[k].astype(F32), g_ref[...])
            project(i)

        project(own)
        project(own + 2)
        wait_for(bias.at[0, 0, pl.ds(0, near - 1)], z_recv.at[t, 0])
        to_neighbours(t, bias, 0)
        if t == 1:
            wait_for(raw.at[pl.ds(other, ROWS)], t_recv.at[2])
            finish(other)
        wait_for(part_of(bias, 0, 0), z_recv.at[t, 1])
        to_neighbours(t, bias, 1)
        if t == 1:
            finish(other + 2)

        def unit(n, c):
            if t == 0:
                rel = jnp.where(n < 6, n % 3, 3)
                kind = jnp.where(n < 6, n // 3, n % 2)

                @pl.when(n == 1)
                def _():
                    wait_for(raw.at[pl.ds(other, 2)], t_recv.at[0])
                    finish(other)
                    relay(t, bias, 0)
                    relay(t, bias, 1)

                @pl.when(n == 3)
                def _():
                    wait_for(raw.at[pl.ds(other + 2, 2)], t_recv.at[1])
                    finish(other + 2)

            else:
                rel, kind = n // 2, n % 2

                @pl.when(n == 2)
                def _():
                    relay(t, bias, 0)
                    relay(t, bias, 1)

            @pl.when(n == 6)
            def _():
                from_far(t, bias, 0)
                from_far(t, bias, 1)

            p = lax.rem(x + (rel ^ (rel >> 1)), nx)
            side = (cls + kind) % 2
            base = ROWS * side
            for r in range(ROWS):
                for k in range(per):
                    part = slice(k * CH, (k + 1) * CH)
                    add = bias[p, k // nz, k % nz].astype(F32)
                    s = score_s[base + r, p, part, :] + add
                    e_s[r, part, :] = jnp.exp2(s - jnp.max(s, axis=-1, keepdims=True)).astype(BF16)
                out = mm(e_s[r], v_s[base + r])
                top_s[r] = out[:, :width]
                low_s[r] = out[:, width:]
            hid = []
            for r in range(ROWS):
                top = top_s[r, pl.ds(0, quer, stride=HEADS), :]
                low = low_s[r, pl.ds(0, quer, stride=HEADS), :]
                for h in range(1, HEADS):
                    rows = pl.ds(h, quer, stride=HEADS)
                    top = jnp.where(lane_head == h, top_s[r, rows, :], top)
                    low = jnp.where(lane_head == h, low_s[r, rows, :], low)
                hid.append((gate_s[base + r, p] * (top / low)).astype(BF16))
            u = mm(jnp.concatenate(hid, axis=0), o_ref[...])
            if t == 1:
                u = u.astype(BF16).astype(F32)
            for r in range(ROWS):
                turn_s[pl.ds(r, quer, stride=ROWS), :] = (
                    res_s[base + r, p] + u[r * quer : (r + 1) * quer]
                )
            stage[pl.ds(p * per, per), side] = turn_s[...].astype(BF16).reshape(per, CH, width)

            def send(k):
                m = p * per + lax.rem(mine + k, per)
                remote(
                    stage.at[m, side], recv.at[mine, side], a_send.at[t], a_recv.at[t, rel],
                    member(m),
                ).start()

            for k in range(1, per):
                send(k)

            @pl.when(rel == 0)
            def _():
                recv[mine, side] = stage[mine, side]

            @pl.when(rel > 0)
            def _():
                send(0)

            return c

        lax.fori_loop(0, 8, unit, 0)

    def taken(t, recv, n):
        p = (x, down, up, far)[n]
        wait_for(recv.at[pl.ds(0, per - (n == 0))], a_recv.at[t, n])
        return p, recv[pl.ds(p * per, per)].reshape(per * 2 * CH, width)

    def in_lanes(part, pieces):
        rows = part.shape[0] // pieces
        return jnp.concatenate([part[i * rows : (i + 1) * rows] for i in range(pieces)], axis=1)

    def arrive(n):
        p, part = taken(0, recv0_s, n)
        here = pl.ds(pl.multiple_of(p * span, span), span)
        four = 4 * 2 * CH
        rows = four // ROWS
        o, i = iota((four, four), 0), iota((four, four), 1)
        order = (o % rows) // ROWS * CH + o // rows * ROWS + o % ROWS
        part = mm(one_hot(order == i), in_lanes(part, per // 4))
        total = None
        for r in range(ROWS):
            row = jnp.concatenate(
                [
                    part[r * rows : (r + 1) * rows, k * width : (k + 1) * width]
                    for k in range(per // 4)
                ],
                axis=0,
            )
            raw1_s[own + r, here, :] = row.astype(BF16)
            normed = ln(row, eg_ref[...])
            x_s[own + r, here, :] = normed
            term = nt(head_rows(eb_ref, r), normed)
            total = term if total is None else total + term
        piece = raw1_s.at[pl.ds(own, ROWS), here, :]
        remote(piece, piece, t_send.at[1], t_recv.at[2], partner).start()
        order = given(p * span + iota((count, span), 1))
        order = one_hot(iota((count, span), 0) == order)
        mask = mm(jnp.broadcast_to(mask_ref[...].astype(F32).astype(BF16), (CH, count)), order)
        bias1_s[x, yi, z, :, here] = (total * LOG2E + (mask - 1.0) * far_mask).astype(BF16)

    def drain(t, raw, bias, stage):
        wait_for(raw.at[pl.ds(own, ROWS)], t_send.at[t])
        wait_for(bias.at[0, 0, pl.ds(0, near - 1)], z_send.at[t])
        wait_for(part_of(bias, 0, 0), z_send.at[t])
        wait_for(bias.at[pl.ds(0, 3)], x_send.at[t])
        wait_for(stage.at[pl.ds(0, members - 1)], a_send.at[t])

    for r in range(ROWS):
        raw0_s[own + r] = pair_ref[r]
    v_s[:, :, width:] = jnp.ones((TEAM, count, width), BF16)
    total = None
    for r in range(ROWS):
        normed = ln(pair_ref[r].astype(F32), sg_ref[...])
        x_s[own + r] = normed
        term = nt(head_rows(sb_ref, r), normed)
        total = term if total is None else total + term
    mask = mask_ref[...].astype(F32)
    bias0_s[x, yi, z] = (total * LOG2E + (mask - 1.0) * far_mask).astype(BF16)
    pl.semaphore_wait(barrier, members)
    gather_plane(0, bias0_s)
    for i in range(2):
        rows = raw0_s.at[pl.ds(own + 2 * i, 2)]
        remote(rows, rows, t_send.at[0], t_recv.at[i], partner).start()

    update(0, sg_ref, sp_ref, so_ref, raw0_s, bias0_s, stage0_s, recv0_s)
    arrive(0)
    arrive(1)
    arrive(2)
    arrive(3)
    gather_plane(1, bias1_s)
    update(1, eg_ref, ep_ref, eo_ref, raw1_s, bias1_s, stage1_s, recv1_s)
    line = nz * 2 * CH
    rows = line // ROWS
    o, i = iota((line, line), 0), iota((line, line), 1)
    order = (o % rows) // ROWS
    order = ((order % nz) * 2 + order // nz) * CH + o // rows * ROWS + o % ROWS
    order = one_hot(order == i)
    for n in range(nx):
        p, part = taken(1, recv1_s, n)
        part = mm(order, in_lanes(part, nyi)).astype(BF16)
        for k in range(nyi):
            here = pl.ds(pl.multiple_of(p * span + k * group, group), group)
            for r in range(ROWS):
                out_ref[r, here, :] = part[
                    r * rows : (r + 1) * rows, k * width : (k + 1) * width
                ]
    drain(0, raw0_s, bias0_s, stage0_s)
    drain(1, raw1_s, bias1_s, stage1_s)


def solution(mesh):
    n = mesh.shape["row"]
    dims = (4, 4, n // 16)

    def body(pair, token_mask, sg, sp, sb, so, eg, ep, eb, eo):
        rows, count, width = pair.shape
        nx, ny, nz = dims
        near, members = ny // 2 * (nz // 2), n // 2
        per = 2 * near
        quer, span = per * ROWS, per * TEAM
        tall = quer * HEADS
        vmem = pl.BlockSpec(memory_space=pltpu.VMEM)
        dma = pltpu.SemaphoreType.DMA
        return pl.pallas_call(
            functools.partial(kernel, dims),
            out_shape=jax.ShapeDtypeStruct(pair.shape, BF16),
            in_specs=[vmem] * 10,
            out_specs=vmem,
            scratch_shapes=[
                pltpu.VMEM((TEAM, count, width), BF16),
                pltpu.VMEM((TEAM, count, width), BF16),
                pltpu.VMEM((TEAM, count, width), BF16),
                pltpu.VMEM((TEAM, count, 2 * width), BF16),
                pltpu.VMEM((TEAM, nx, tall, count), F32),
                pltpu.VMEM((TEAM, nx, quer, width), F32),
                pltpu.VMEM((TEAM, nx, quer, width), F32),
                pltpu.VMEM((ROWS, tall, count), BF16),
                pltpu.VMEM((ROWS, tall, width), F32),
                pltpu.VMEM((ROWS, tall, width), F32),
                pltpu.VMEM((quer * ROWS, width), F32),
                pltpu.VMEM((nx, ny // 2, nz, CH, count), BF16),
                pltpu.VMEM((nx, ny // 2, nz, CH, count), BF16),
                pltpu.VMEM((members, 2, CH, width), BF16),
                pltpu.VMEM((members, 2, CH, width), BF16),
                pltpu.VMEM((members, 2, CH, width), BF16),
                pltpu.VMEM((members, 2, CH, width), BF16),
                pltpu.VMEM((quer, span), BF16),
                pltpu.VMEM((tall, quer), BF16),
                pltpu.VMEM((width, 2 * width), BF16),
                pltpu.VMEM((width, 2 * width), BF16),
                pltpu.VMEM((2, nx * tall, width), BF16),
                dma((2,)), dma((3,)), dma((2,)), dma((2, 2)),
                dma((2,)), dma((2, 8)), dma((2,)), dma((2, 4)),
            ],
            compiler_params=pltpu.CompilerParams(
                collective_id=0, has_side_effects=True, vmem_limit_bytes=60 * 1024 * 1024
            ),
        )(
            pair, token_mask.reshape(1, count), sg.reshape(1, width), sp, sb.T, so,
            eg.reshape(1, width), ep, eb.T, eo,
        )

    return jax.shard_map(
        body,
        mesh=mesh,
        in_specs=(P(("rep", "row"), None, None), P("rep"), P(), P(), P(), P(), P(), P(), P(), P()),
        out_specs=P(("rep", "row"), None, None),
        check_vma=False,
    )
```

```python
import functools
import math

import jax
import jax.numpy as jnp
from jax import lax
from jax.experimental import pallas as pl
from jax.experimental.pallas import tpu as pltpu
from jax.sharding import PartitionSpec as P

MESH = pl.DeviceIdType.MESH
LOG2E = 1.4426950408889634
F32 = jnp.float32
BF16 = jnp.bfloat16
ROWS = 4
TEAM = 2 * ROWS
HEADS = 4
CH = ROWS * HEADS


def iota(shape, dim):
    return lax.broadcasted_iota(jnp.int32, shape, dim)


def one_hot(cond):
    return cond.astype(F32).astype(BF16)


def nt(a, b):
    return lax.dot_general(a, b, (((1,), (1,)), ((), ())), preferred_element_type=F32)


def mm(a, b):
    return jnp.dot(a, b, preferred_element_type=F32)


def ln(wide, gain):
    center = wide - jnp.mean(wide, axis=-1, keepdims=True)
    spread = jnp.mean(center * center, axis=-1, keepdims=True)
    return (center * lax.rsqrt(spread + 1e-05) * gain).astype(BF16)


def kernel(
    dims,
    pair_ref, mask_ref, sg_ref, sp_ref, sb_ref, so_ref, eg_ref, ep_ref, eb_ref, eo_ref,
    out_ref,
    raw0_s, raw1_s, x_s, v_s, score_s, gate_s, res_s, e_s, top_s, low_s, turn_s,
    bias0_s, bias1_s, stage0_s, stage1_s, recv0_s, recv1_s, pick_s, spread_s, wkv_s, wqg_s, q_s, mask_s,
    t_send, t_recv, z_send, z_recv, x_send, x_recv, a_send, a_recv,
):
    nx, ny, nz = dims
    nyi, nzh = ny // 2, nz // 2
    near = nyi * nzh
    per = 2 * near
    members = nx * per
    me = lax.axis_index("row")
    x, y, z = me // (ny * nz), (me // nz) % ny, me % nz
    cls, yi = y % 2, y // 2
    hz, local = z // nzh, yi * nzh + z % nzh
    mine = (x * nyi + yi) * nz + z
    width = x_s.shape[2]
    count = x_s.shape[1]
    size = width // HEADS
    quer = per * ROWS
    tall = quer * HEADS
    span = per * TEAM
    group = nz * TEAM

    barrier = pltpu.get_barrier_semaphore()

    def greet_one(peer):
        pl.semaphore_signal(barrier, inc=1, device_id={"row": peer}, device_id_type=MESH)

    def member(m):
        return (2 * (m // nz) + cls) * nz + m % nz

    def place(p, half, i):
        return (p * nyi + i // nzh) * nz + half * nzh + i % nzh

    partner = me + nz * (1 - 2 * cls)
    greet_one(partner)

    def greet(s, c):
        greet_one(member(lax.rem(mine + s, members)))
        return c

    lax.fori_loop(1, members, greet, 0)

    def remote(src, dst, send, recv, peer):
        return pltpu.make_async_remote_copy(
            src_ref=src, dst_ref=dst, send_sem=send, recv_sem=recv,
            device_id={"row": peer}, device_id_type=MESH,
        )

    def wait_for(view, sem):
        pltpu.make_async_copy(view, view, sem).wait()

    def given(token):
        rest = token % group
        return token - rest + (rest // ROWS) % 2 * (nz * ROWS) + rest // TEAM * ROWS + rest % ROWS

    lane_head = iota((quer, width), 1) // size
    head = (iota((tall, width), 0) % HEADS == iota((tall, width), 1) // size).astype(F32)
    far_mask = 1e9 * LOG2E

    own = ROWS * cls
    other = ROWS - own
    up, down, far = lax.rem(x + 1, nx), lax.rem(x + nx - 1, nx), lax.rem(x + 2, nx)
    to_up = member(mine + (up - x) * per)
    to_down = member(mine + (down - x) * per)

    def part_of(bias, p, late):
        half = (hz + late) % 2
        return bias.at[p, :, pl.ds(half * nzh, nzh)]

    def quarter(bias, p, i, late):
        half = (hz + late) % 2
        return bias.at[p, i, pl.ds(half * nzh, nzh)]

    def head_rows(b_ref, r):
        a, b = iota((CH, HEADS), 0), iota((CH, HEADS), 1)
        return mm(one_hot((a // HEADS == r) & (a % HEADS == b)), b_ref[...]).astype(BF16)

    def gather_plane(t, bias):
        for late in range(2):

            def go(s, c):
                peer = member(place(x, (hz + late) % 2, lax.rem(local + s, near)))
                share = bias.at[x, yi, z]
                remote(share, share, z_send.at[t], z_recv.at[t, late], peer).start()
                return c

            lax.fori_loop(1 - late, near, go, 0)

    def to_neighbours(t, bias, late):
        part = part_of(bias, x, late)
        remote(part, part, x_send.at[t], x_recv.at[t, late], to_down).start()
        remote(part, part, x_send.at[t], x_recv.at[t, 2 + late], to_up).start()

    def relay(t, bias, late):
        wait_for(part_of(bias, up, late), x_recv.at[t, late])
        part = quarter(bias, up, 0, late)
        remote(part, part, x_send.at[t], x_recv.at[t, 4 + late], to_down).start()
        wait_for(part_of(bias, down, late), x_recv.at[t, 2 + late])
        part = quarter(bias, down, 1, late)
        remote(part, part, x_send.at[t], x_recv.at[t, 6 + late], to_up).start()

    def from_far(t, bias, late):
        wait_for(quarter(bias, far, 0, late), x_recv.at[t, 4 + late])
        wait_for(quarter(bias, far, 1, late), x_recv.at[t, 6 + late])

    def constants(t, p_ref):
        row, col = iota((quer, span), 0), iota((quer, span), 1)
        token = row // ROWS * TEAM + ROWS * cls + row % ROWS
        pick_s[...] = one_hot((given(token) if t == 0 else token) == col)
        wkv_s[...] = p_ref[:, width : 3 * width]
        wqg_s[:, :width] = p_ref[:, :width]
        wqg_s[:, width:] = p_ref[:, 3 * width :]

    def update(t, g_ref, o_ref, raw, bias, stage, recv):
        def project(i):
            pair = (i, i + 1)
            kv = [mm(x_s[k], wkv_s[...]) for k in pair]
            keys = [a[:, :width].astype(BF16) for a in kv]
            for k, a in zip(pair, kv):
                v_s[k, :, :width] = a[:, width:].astype(BF16)
            for p in range(nx):
                part = slice(p * span, (p + 1) * span)
                both = jnp.concatenate(
                    [x_s[i, part, :], x_s[i + 1, part, :], raw[i, part, :], raw[i + 1, part, :]],
                    axis=1,
                )
                both = mm(pick_s[...], both)
                normed = both[:, : 2 * width].astype(BF16)
                normed = jnp.concatenate([normed[:, :width], normed[:, width:]], axis=0)
                qg = mm(normed, wqg_s[...])
                gate = jax.nn.sigmoid(qg[:, width:].astype(BF16).astype(F32))
                q = (qg[:, :width] * (LOG2E / math.sqrt(size))).astype(BF16)
                q = mm(spread_s[...], jnp.concatenate([q[:quer], q[quer:]], axis=1))
                for n, k in enumerate(pair):
                    res_s[k, p] = both[:, (2 + n) * width : (3 + n) * width]
                    gate_s[k, p] = gate[n * quer : (n + 1) * quer]
                    one = q[:, n * width : (n + 1) * width] * head
                    q_s[n, p * tall : (p + 1) * tall, :] = one.astype(BF16)
            for n, k in enumerate(pair):
                score_s[k] = nt(q_s[n], keys[n]).reshape(nx, tall, count)

        def finish(i):
            for k in (i, i + 1):
                x_s[k] = ln(raw[k].astype(F32), g_ref[...])
            project(i)

        project(own)
        project(own + 2)
        wait_for(bias.at[0, 0, pl.ds(0, near - 1)], z_recv.at[t, 0])
        to_neighbours(t, bias, 0)
        if t == 1:
            wait_for(raw.at[pl.ds(other, ROWS)], t_recv.at[2])
            finish(other)
        wait_for(part_of(bias, 0, 0), z_recv.at[t, 1])
        to_neighbours(t, bias, 1)
        if t == 1:
            finish(other + 2)

        def unit(n, c):
            if t == 0:
                rel = jnp.where(n < 6, n % 3, 3)
                kind = jnp.where(n < 6, n // 3, n % 2)

                @pl.when(n == 1)
                def _():
                    wait_for(raw.at[pl.ds(other, 2)], t_recv.at[0])
                    finish(other)
                    relay(t, bias, 0)
                    relay(t, bias, 1)

                @pl.when(n == 3)
                def _():
                    wait_for(raw.at[pl.ds(other + 2, 2)], t_recv.at[1])
                    finish(other + 2)

            else:
                rel, kind = n // 2, n % 2

                @pl.when(n == 2)
                def _():
                    relay(t, bias, 0)
                    relay(t, bias, 1)

            @pl.when(n == 6)
            def _():
                from_far(t, bias, 0)
                from_far(t, bias, 1)

            p = lax.rem(x + (rel ^ (rel >> 1)), nx)
            side = (cls + kind) % 2
            base = ROWS * side
            for r in range(ROWS):
                for k in range(per):
                    part = slice(k * CH, (k + 1) * CH)
                    add = bias[p, k // nz, k % nz].astype(F32)
                    s = score_s[base + r, p, part, :] + add
                    e_s[r, part, :] = jnp.exp2(s - jnp.max(s, axis=-1, keepdims=True)).astype(BF16)
                out = mm(e_s[r], v_s[base + r])
                top_s[r] = out[:, :width]
                low_s[r] = out[:, width:]
            hid = []
            for r in range(ROWS):
                top = top_s[r, pl.ds(0, quer, stride=HEADS), :]
                low = low_s[r, pl.ds(0, quer, stride=HEADS), :]
                for h in range(1, HEADS):
                    rows = pl.ds(h, quer, stride=HEADS)
                    top = jnp.where(lane_head == h, top_s[r, rows, :], top)
                    low = jnp.where(lane_head == h, low_s[r, rows, :], low)
                hid.append((gate_s[base + r, p] * (top / low)).astype(BF16))
            u = mm(jnp.concatenate(hid, axis=0), o_ref[...])
            if t == 1:
                u = u.astype(BF16).astype(F32)
            for r in range(ROWS):
                turn_s[pl.ds(r, quer, stride=ROWS), :] = (
                    res_s[base + r, p] + u[r * quer : (r + 1) * quer]
                )
            stage[pl.ds(p * per, per), side] = turn_s[...].astype(BF16).reshape(per, CH, width)

            def send(k):
                m = p * per + lax.rem(mine + k, per)
                remote(
                    stage.at[m, side], recv.at[mine, side], a_send.at[t], a_recv.at[t, rel],
                    member(m),
                ).start()

            for k in range(1, per):
                send(k)

            @pl.when(rel == 0)
            def _():
                recv[mine, side] = stage[mine, side]

            @pl.when(rel > 0)
            def _():
                send(0)

            return c

        lax.fori_loop(0, 8, unit, 0)

    def taken(t, recv, n):
        p = (x, down, up, far)[n]
        wait_for(recv.at[pl.ds(0, per - (n == 0))], a_recv.at[t, n])
        return p, recv[pl.ds(p * per, per)].reshape(per * 2 * CH, width)

    def in_lanes(part, pieces):
        rows = part.shape[0] // pieces
        return jnp.concatenate([part[i * rows : (i + 1) * rows] for i in range(pieces)], axis=1)

    def arrive(n):
        p, part = taken(0, recv0_s, n)
        here = pl.ds(pl.multiple_of(p * span, span), span)
        four = 4 * 2 * CH
        rows = four // ROWS
        o, i = iota((four, four), 0), iota((four, four), 1)
        order = (o % rows) // ROWS * CH + o // rows * ROWS + o % ROWS
        part = mm(one_hot(order == i), in_lanes(part, per // 4))
        total = None
        for r in range(ROWS):
            row = jnp.concatenate(
                [
                    part[r * rows : (r + 1) * rows, k * width : (k + 1) * width]
                    for k in range(per // 4)
                ],
                axis=0,
            )
            raw1_s[own + r, here, :] = row.astype(BF16)
            normed = ln(row, eg_ref[...])
            x_s[own + r, here, :] = normed
            term = nt(head_rows(eb_ref, r), normed)
            total = term if total is None else total + term
        piece = raw1_s.at[pl.ds(own, ROWS), here, :]
        remote(piece, piece, t_send.at[1], t_recv.at[2], partner).start()
        bias1_s[x, yi, z, :, here] = (total * LOG2E + mask_s[:, here]).astype(BF16)

    def drain(t, raw, bias, stage):
        wait_for(raw.at[pl.ds(own, ROWS)], t_send.at[t])
        wait_for(bias.at[0, 0, pl.ds(0, near - 1)], z_send.at[t])
        wait_for(part_of(bias, 0, 0), z_send.at[t])
        wait_for(bias.at[pl.ds(0, 3)], x_send.at[t])
        wait_for(stage.at[pl.ds(0, members - 1)], a_send.at[t])

    total = None
    for r in range(ROWS):
        normed = ln(pair_ref[r].astype(F32), sg_ref[...])
        x_s[own + r] = normed
        term = nt(head_rows(sb_ref, r), normed)
        total = term if total is None else total + term
    mask = mask_ref[...].astype(F32)
    bias0_s[x, yi, z] = (total * LOG2E + (mask - 1.0) * far_mask).astype(BF16)
    pl.semaphore_wait(barrier, members)
    gather_plane(0, bias0_s)
    for i in range(2):
        remote(
            pair_ref.at[pl.ds(2 * i, 2)], raw0_s.at[pl.ds(own + 2 * i, 2)],
            t_send.at[0], t_recv.at[i], partner,
        ).start()
    for r in range(ROWS):
        raw0_s[own + r] = pair_ref[r]
    v_s[:, :, width:] = jnp.ones((TEAM, count, width), BF16)
    spread_s[...] = one_hot(iota((tall, quer), 0) // HEADS == iota((tall, quer), 1))
    constants(0, sp_ref)

    update(0, sg_ref, so_ref, raw0_s, bias0_s, stage0_s, recv0_s)
    constants(1, ep_ref)
    order = one_hot(iota((count, count), 0) == given(iota((count, count), 1)))
    mask = mm(jnp.broadcast_to(mask_ref[...].astype(F32).astype(BF16), (CH, count)), order)
    mask_s[...] = (mask - 1.0) * far_mask
    for n in range(nx):
        arrive(n)
    gather_plane(1, bias1_s)
    update(1, eg_ref, eo_ref, raw1_s, bias1_s, stage1_s, recv1_s)
    line = nz * 2 * CH
    rows = line // ROWS
    o, i = iota((line, line), 0), iota((line, line), 1)
    order = (o % rows) // ROWS
    order = ((order % nz) * 2 + order // nz) * CH + o // rows * ROWS + o % ROWS
    order = one_hot(order == i)
    for n in range(nx):
        p, part = taken(1, recv1_s, n)
        part = mm(order, in_lanes(part, nyi))
        for k in range(nyi):
            here = pl.ds(pl.multiple_of(p * span + k * group, group), group)
            for r in range(ROWS):
                out_ref[r, here, :] = part[
                    r * rows : (r + 1) * rows, k * width : (k + 1) * width
                ]
    drain(0, raw0_s, bias0_s, stage0_s)
    drain(1, raw1_s, bias1_s, stage1_s)


def solution(mesh):
    n = mesh.shape["row"]
    dims = (4, 4, n // 16)

    def body(pair, token_mask, sg, sp, sb, so, eg, ep, eb, eo):
        rows, count, width = pair.shape
        nx, ny, nz = dims
        near, members = ny // 2 * (nz // 2), n // 2
        per = 2 * near
        quer, span = per * ROWS, per * TEAM
        tall = quer * HEADS
        vmem = pl.BlockSpec(memory_space=pltpu.VMEM)
        dma = pltpu.SemaphoreType.DMA
        return pl.pallas_call(
            functools.partial(kernel, dims),
            out_shape=jax.ShapeDtypeStruct(pair.shape, F32),
            in_specs=[vmem] * 10,
            out_specs=vmem,
            scratch_shapes=[
                pltpu.VMEM((TEAM, count, width), BF16),
                pltpu.VMEM((TEAM, count, width), BF16),
                pltpu.VMEM((TEAM, count, width), BF16),
                pltpu.VMEM((TEAM, count, 2 * width), BF16),
                pltpu.VMEM((TEAM, nx, tall, count), F32),
                pltpu.VMEM((TEAM, nx, quer, width), F32),
                pltpu.VMEM((TEAM, nx, quer, width), F32),
                pltpu.VMEM((ROWS, tall, count), BF16),
                pltpu.VMEM((ROWS, tall, width), F32),
                pltpu.VMEM((ROWS, tall, width), F32),
                pltpu.VMEM((quer * ROWS, width), F32),
                pltpu.VMEM((nx, ny // 2, nz, CH, count), BF16),
                pltpu.VMEM((nx, ny // 2, nz, CH, count), BF16),
                pltpu.VMEM((members, 2, CH, width), BF16),
                pltpu.VMEM((members, 2, CH, width), BF16),
                pltpu.VMEM((members, 2, CH, width), BF16),
                pltpu.VMEM((members, 2, CH, width), BF16),
                pltpu.VMEM((quer, span), BF16),
                pltpu.VMEM((tall, quer), BF16),
                pltpu.VMEM((width, 2 * width), BF16),
                pltpu.VMEM((width, 2 * width), BF16),
                pltpu.VMEM((2, nx * tall, width), BF16),
                pltpu.VMEM((CH, count), F32),
                dma((2,)), dma((3,)), dma((2,)), dma((2, 2)),
                dma((2,)), dma((2, 8)), dma((2,)), dma((2, 4)),
            ],
            compiler_params=pltpu.CompilerParams(
                collective_id=0, has_side_effects=True, vmem_limit_bytes=60 * 1024 * 1024
            ),
        )(
            pair, token_mask.reshape(1, count), sg.reshape(1, width), sp, sb.T, so,
            eg.reshape(1, width), ep, eb.T, eo,
        ).astype(BF16)

    return jax.shard_map(
        body,
        mesh=mesh,
        in_specs=(P(("rep", "row"), None, None), P("rep"), P(), P(), P(), P(), P(), P(), P(), P()),
        out_specs=P(("rep", "row"), None, None),
        check_vma=False,
    )
```

```python
import functools
import math

import jax
import jax.numpy as jnp
from jax import lax
from jax.experimental import pallas as pl
from jax.experimental.pallas import tpu as pltpu
from jax.sharding import PartitionSpec as P

MESH = pl.DeviceIdType.MESH
LOG2E = 1.4426950408889634
F32 = jnp.float32
BF16 = jnp.bfloat16
ROWS = 4
TEAM = 2 * ROWS
HEADS = 4
CH = ROWS * HEADS


def iota(shape, dim):
    return lax.broadcasted_iota(jnp.int32, shape, dim)


def one_hot(cond):
    return cond.astype(F32).astype(BF16)


def nt(a, b):
    return lax.dot_general(a, b, (((1,), (1,)), ((), ())), preferred_element_type=F32)


def mm(a, b):
    return jnp.dot(a, b, preferred_element_type=F32)


def ln(wide, gain):
    center = wide - jnp.mean(wide, axis=-1, keepdims=True)
    spread = jnp.mean(center * center, axis=-1, keepdims=True)
    return (center * lax.rsqrt(spread + 1e-05) * gain).astype(BF16)


def kernel(
    dims,
    pair_in, mask_in, sg_in, sp_in, sb_in, so_in, eg_in, ep_in, eb_in, eo_in,
    out_ref,
    mask_ref, sg_ref, sp_ref, sb_ref, so_ref, eg_ref, ep_ref, eb_ref, eo_ref, load_sem,
    raw0_s, raw1_s, x_s, v_s, score_s, gate_s, res_s, e_s, top_s, low_s, turn_s,
    bias0_s, bias1_s, stage0_s, stage1_s, recv0_s, recv1_s, pick_s, spread_s, wkv_s, wqg_s, q_s, mask_s,
    t_send, t_recv, z_send, z_recv, x_send, x_recv, a_send, a_recv,
):
    nx, ny, nz = dims
    nyi, nzh = ny // 2, nz // 2
    near = nyi * nzh
    per = 2 * near
    members = nx * per
    me = lax.axis_index("row")
    x, y, z = me // (ny * nz), (me // nz) % ny, me % nz
    cls, yi = y % 2, y // 2
    hz, local = z // nzh, yi * nzh + z % nzh
    mine = (x * nyi + yi) * nz + z
    width = x_s.shape[2]
    count = x_s.shape[1]
    size = width // HEADS
    quer = per * ROWS
    tall = quer * HEADS
    span = per * TEAM
    group = nz * TEAM

    own = ROWS * cls
    other = ROWS - own
    own_rows = raw0_s.at[pl.ds(own, ROWS)]
    loads = (
        (pair_in, own_rows), (sg_in, sg_ref), (sb_in, sb_ref), (mask_in, mask_ref),
        (sp_in, sp_ref), (so_in, so_ref), (eg_in, eg_ref), (ep_in, ep_ref), (eb_in, eb_ref),
        (eo_in, eo_ref),
    )
    loads = [pltpu.make_async_copy(a, b, load_sem.at[i]) for i, (a, b) in enumerate(loads)]
    for load in loads:
        load.start()

    barrier = pltpu.get_barrier_semaphore()

    def greet_one(peer):
        pl.semaphore_signal(barrier, inc=1, device_id={"row": peer}, device_id_type=MESH)

    def member(m):
        return (2 * (m // nz) + cls) * nz + m % nz

    def place(p, half, i):
        return (p * nyi + i // nzh) * nz + half * nzh + i % nzh

    partner = me + nz * (1 - 2 * cls)
    greet_one(partner)

    def greet(s, c):
        greet_one(member(lax.rem(mine + s, members)))
        return c

    lax.fori_loop(1, members, greet, 0)

    def remote(src, dst, send, recv, peer):
        return pltpu.make_async_remote_copy(
            src_ref=src, dst_ref=dst, send_sem=send, recv_sem=recv,
            device_id={"row": peer}, device_id_type=MESH,
        )

    def wait_for(view, sem):
        pltpu.make_async_copy(view, view, sem).wait()

    def given(token):
        rest = token % group
        return token - rest + (rest // ROWS) % 2 * (nz * ROWS) + rest // TEAM * ROWS + rest % ROWS

    lane_head = iota((quer, width), 1) // size
    head = (iota((tall, width), 0) % HEADS == iota((tall, width), 1) // size).astype(F32)
    far_mask = 1e9 * LOG2E

    up, down, far = lax.rem(x + 1, nx), lax.rem(x + nx - 1, nx), lax.rem(x + 2, nx)
    to_up = member(mine + (up - x) * per)
    to_down = member(mine + (down - x) * per)

    def part_of(bias, p, late):
        half = (hz + late) % 2
        return bias.at[p, :, pl.ds(half * nzh, nzh)]

    def quarter(bias, p, i, late):
        half = (hz + late) % 2
        return bias.at[p, i, pl.ds(half * nzh, nzh)]

    def head_rows(b_ref, r):
        a, b = iota((CH, HEADS), 0), iota((CH, HEADS), 1)
        return mm(one_hot((a // HEADS == r) & (a % HEADS == b)), b_ref[...]).astype(BF16)

    def gather_plane(t, bias):
        for late in range(2):

            def go(s, c):
                peer = member(place(x, (hz + late) % 2, lax.rem(local + s, near)))
                share = bias.at[x, yi, z]
                remote(share, share, z_send.at[t], z_recv.at[t, late], peer).start()
                return c

            lax.fori_loop(1 - late, near, go, 0)

    def to_neighbours(t, bias, late):
        part = part_of(bias, x, late)
        remote(part, part, x_send.at[t], x_recv.at[t, late], to_down).start()
        remote(part, part, x_send.at[t], x_recv.at[t, 2 + late], to_up).start()

    def relay(t, bias, late):
        wait_for(part_of(bias, up, late), x_recv.at[t, late])
        part = quarter(bias, up, 0, late)
        remote(part, part, x_send.at[t], x_recv.at[t, 4 + late], to_down).start()
        wait_for(part_of(bias, down, late), x_recv.at[t, 2 + late])
        part = quarter(bias, down, 1, late)
        remote(part, part, x_send.at[t], x_recv.at[t, 6 + late], to_up).start()

    def from_far(t, bias, late):
        wait_for(quarter(bias, far, 0, late), x_recv.at[t, 4 + late])
        wait_for(quarter(bias, far, 1, late), x_recv.at[t, 6 + late])

    def constants(t, p_ref):
        row, col = iota((quer, span), 0), iota((quer, span), 1)
        token = row // ROWS * TEAM + ROWS * cls + row % ROWS
        pick_s[...] = one_hot((given(token) if t == 0 else token) == col)
        wkv_s[...] = p_ref[:, width : 3 * width]
        wqg_s[:, :width] = p_ref[:, :width]
        wqg_s[:, width:] = p_ref[:, 3 * width :]

    def update(t, g_ref, o_ref, raw, bias, stage, recv):
        def project(i):
            pair = (i, i + 1)
            kv = [mm(x_s[k], wkv_s[...]) for k in pair]
            keys = [a[:, :width].astype(BF16) for a in kv]
            for k, a in zip(pair, kv):
                v_s[k, :, :width] = a[:, width:].astype(BF16)
            for p in range(nx):
                part = slice(p * span, (p + 1) * span)
                both = jnp.concatenate(
                    [x_s[i, part, :], x_s[i + 1, part, :], raw[i, part, :], raw[i + 1, part, :]],
                    axis=1,
                )
                both = mm(pick_s[...], both)
                normed = both[:, : 2 * width].astype(BF16)
                normed = jnp.concatenate([normed[:, :width], normed[:, width:]], axis=0)
                qg = mm(normed, wqg_s[...])
                gate = jax.nn.sigmoid(qg[:, width:].astype(BF16).astype(F32))
                q = (qg[:, :width] * (LOG2E / math.sqrt(size))).astype(BF16)
                q = mm(spread_s[...], jnp.concatenate([q[:quer], q[quer:]], axis=1))
                for n, k in enumerate(pair):
                    res_s[k, p] = both[:, (2 + n) * width : (3 + n) * width]
                    gate_s[k, p] = gate[n * quer : (n + 1) * quer]
                    one = q[:, n * width : (n + 1) * width] * head
                    q_s[n, p * tall : (p + 1) * tall, :] = one.astype(BF16)
            for n, k in enumerate(pair):
                score_s[k] = nt(q_s[n], keys[n]).reshape(nx, tall, count)

        def finish(i):
            for k in (i, i + 1):
                x_s[k] = ln(raw[k].astype(F32), g_ref[...])
            project(i)

        project(own)
        project(own + 2)
        wait_for(bias.at[0, 0, pl.ds(0, near - 1)], z_recv.at[t, 0])
        to_neighbours(t, bias, 0)
        if t == 1:
            wait_for(raw.at[pl.ds(other, ROWS)], t_recv.at[2])
            finish(other)
        wait_for(part_of(bias, 0, 0), z_recv.at[t, 1])
        to_neighbours(t, bias, 1)
        if t == 1:
            finish(other + 2)

        def unit(n, c):
            if t == 0:
                rel = jnp.where(n < 6, n % 3, 3)
                kind = jnp.where(n < 6, n // 3, n % 2)

                @pl.when(n == 1)
                def _():
                    wait_for(raw.at[pl.ds(other, 2)], t_recv.at[0])
                    finish(other)
                    relay(t, bias, 0)
                    relay(t, bias, 1)

                @pl.when(n == 3)
                def _():
                    wait_for(raw.at[pl.ds(other + 2, 2)], t_recv.at[1])
                    finish(other + 2)

            else:
                rel, kind = n // 2, n % 2

                @pl.when(n == 2)
                def _():
                    relay(t, bias, 0)
                    relay(t, bias, 1)

            @pl.when(n == 6)
            def _():
                from_far(t, bias, 0)
                from_far(t, bias, 1)

            p = lax.rem(x + (rel ^ (rel >> 1)), nx)
            side = (cls + kind) % 2
            base = ROWS * side
            for r in range(ROWS):
                for k in range(per):
                    part = slice(k * CH, (k + 1) * CH)
                    add = bias[p, k // nz, k % nz].astype(F32)
                    s = score_s[base + r, p, part, :] + add
                    e_s[r, part, :] = jnp.exp2(s - jnp.max(s, axis=-1, keepdims=True)).astype(BF16)
                out = mm(e_s[r], v_s[base + r])
                top_s[r] = out[:, :width]
                low_s[r] = out[:, width:]
            hid = []
            for r in range(ROWS):
                top = top_s[r, pl.ds(0, quer, stride=HEADS), :]
                low = low_s[r, pl.ds(0, quer, stride=HEADS), :]
                for h in range(1, HEADS):
                    rows = pl.ds(h, quer, stride=HEADS)
                    top = jnp.where(lane_head == h, top_s[r, rows, :], top)
                    low = jnp.where(lane_head == h, low_s[r, rows, :], low)
                hid.append((gate_s[base + r, p] * (top / low)).astype(BF16))
            u = mm(jnp.concatenate(hid, axis=0), o_ref[...])
            if t == 1:
                u = u.astype(BF16).astype(F32)
            for r in range(ROWS):
                turn_s[pl.ds(r, quer, stride=ROWS), :] = (
                    res_s[base + r, p] + u[r * quer : (r + 1) * quer]
                )
            stage[pl.ds(p * per, per), side] = turn_s[...].astype(BF16).reshape(per, CH, width)

            def send(k):
                m = p * per + lax.rem(mine + k, per)
                remote(
                    stage.at[m, side], recv.at[mine, side], a_send.at[t], a_recv.at[t, rel],
                    member(m),
                ).start()

            for k in range(1, per):
                send(k)

            @pl.when(rel == 0)
            def _():
                recv[mine, side] = stage[mine, side]

            @pl.when(rel > 0)
            def _():
                send(0)

            return c

        lax.fori_loop(0, 8, unit, 0)

    def taken(t, recv, n):
        p = (x, down, up, far)[n]
        wait_for(recv.at[pl.ds(0, per - (n == 0))], a_recv.at[t, n])
        return p, recv[pl.ds(p * per, per)].reshape(per * 2 * CH, width)

    def in_lanes(part, pieces):
        rows = part.shape[0] // pieces
        return jnp.concatenate([part[i * rows : (i + 1) * rows] for i in range(pieces)], axis=1)

    def arrive(n):
        p, part = taken(0, recv0_s, n)
        here = pl.ds(pl.multiple_of(p * span, span), span)
        four = 4 * 2 * CH
        rows = four // ROWS
        o, i = iota((four, four), 0), iota((four, four), 1)
        order = (o % rows) // ROWS * CH + o // rows * ROWS + o % ROWS
        part = mm(one_hot(order == i), in_lanes(part, per // 4))
        total = None
        for r in range(ROWS):
            row = jnp.concatenate(
                [
                    part[r * rows : (r + 1) * rows, k * width : (k + 1) * width]
                    for k in range(per // 4)
                ],
                axis=0,
            )
            raw1_s[own + r, here, :] = row.astype(BF16)
            normed = ln(row, eg_ref[...])
            x_s[own + r, here, :] = normed
            term = nt(head_rows(eb_ref, r), normed)
            total = term if total is None else total + term
        piece = raw1_s.at[pl.ds(own, ROWS), here, :]
        remote(piece, piece, t_send.at[1], t_recv.at[2], partner).start()
        bias1_s[x, yi, z, :, here] = (total * LOG2E + mask_s[:, here]).astype(BF16)

    def drain(t, raw, bias, stage):
        wait_for(raw.at[pl.ds(own, ROWS)], t_send.at[t])
        wait_for(bias.at[0, 0, pl.ds(0, near - 1)], z_send.at[t])
        wait_for(part_of(bias, 0, 0), z_send.at[t])
        wait_for(bias.at[pl.ds(0, 3)], x_send.at[t])
        wait_for(stage.at[pl.ds(0, members - 1)], a_send.at[t])

    for load in loads[:4]:
        load.wait()
    total = None
    for r in range(ROWS):
        normed = ln(raw0_s[own + r].astype(F32), sg_ref[...])
        x_s[own + r] = normed
        term = nt(head_rows(sb_ref, r), normed)
        total = term if total is None else total + term
    mask = mask_ref[...].astype(F32)
    bias0_s[x, yi, z] = (total * LOG2E + (mask - 1.0) * far_mask).astype(BF16)
    pl.semaphore_wait(barrier, members)
    gather_plane(0, bias0_s)
    for i in range(2):
        rows = raw0_s.at[pl.ds(own + 2 * i, 2)]
        remote(rows, rows, t_send.at[0], t_recv.at[i], partner).start()
    for load in loads[4:]:
        load.wait()
    v_s[:, :, width:] = jnp.ones((TEAM, count, width), BF16)
    spread_s[...] = one_hot(iota((tall, quer), 0) // HEADS == iota((tall, quer), 1))
    constants(0, sp_ref)

    update(0, sg_ref, so_ref, raw0_s, bias0_s, stage0_s, recv0_s)
    constants(1, ep_ref)
    order = one_hot(iota((count, count), 0) == given(iota((count, count), 1)))
    mask = mm(jnp.broadcast_to(mask_ref[...].astype(F32).astype(BF16), (CH, count)), order)
    mask_s[...] = (mask - 1.0) * far_mask
    for n in range(nx):
        arrive(n)
    gather_plane(1, bias1_s)
    update(1, eg_ref, eo_ref, raw1_s, bias1_s, stage1_s, recv1_s)
    line = nz * 2 * CH
    rows = line // ROWS
    o, i = iota((line, line), 0), iota((line, line), 1)
    order = (o % rows) // ROWS
    order = ((order % nz) * 2 + order // nz) * CH + o // rows * ROWS + o % ROWS
    order = one_hot(order == i)
    for n in range(nx):
        p, part = taken(1, recv1_s, n)
        part = mm(order, in_lanes(part, nyi)).astype(BF16)
        for k in range(nyi):
            here = pl.ds(pl.multiple_of(p * span + k * group, group), group)
            for r in range(ROWS):
                out_ref[r, here, :] = part[
                    r * rows : (r + 1) * rows, k * width : (k + 1) * width
                ]
    drain(0, raw0_s, bias0_s, stage0_s)
    drain(1, raw1_s, bias1_s, stage1_s)


def solution(mesh):
    n = mesh.shape["row"]
    dims = (4, 4, n // 16)

    def body(pair, token_mask, sg, sp, sb, so, eg, ep, eb, eo):
        rows, count, width = pair.shape
        nx, ny, nz = dims
        near, members = ny // 2 * (nz // 2), n // 2
        per = 2 * near
        quer, span = per * ROWS, per * TEAM
        tall = quer * HEADS
        vmem = pl.BlockSpec(memory_space=pltpu.VMEM)
        dma = pltpu.SemaphoreType.DMA
        return pl.pallas_call(
            functools.partial(kernel, dims),
            out_shape=jax.ShapeDtypeStruct(pair.shape, BF16),
            in_specs=[pl.BlockSpec(memory_space=pl.ANY)] * 10,
            out_specs=vmem,
            scratch_shapes=[
                pltpu.VMEM((1, count), jnp.int32),
                *[
                    shape
                    for _ in range(2)
                    for shape in (
                        pltpu.VMEM((1, width), F32),
                        pltpu.VMEM((width, 4 * width), BF16),
                        pltpu.VMEM((HEADS, width), BF16),
                        pltpu.VMEM((width, width), BF16),
                    )
                ],
                dma((10,)),
                pltpu.VMEM((TEAM, count, width), BF16),
                pltpu.VMEM((TEAM, count, width), BF16),
                pltpu.VMEM((TEAM, count, width), BF16),
                pltpu.VMEM((TEAM, count, 2 * width), BF16),
                pltpu.VMEM((TEAM, nx, tall, count), F32),
                pltpu.VMEM((TEAM, nx, quer, width), F32),
                pltpu.VMEM((TEAM, nx, quer, width), F32),
                pltpu.VMEM((ROWS, tall, count), BF16),
                pltpu.VMEM((ROWS, tall, width), F32),
                pltpu.VMEM((ROWS, tall, width), F32),
                pltpu.VMEM((quer * ROWS, width), F32),
                pltpu.VMEM((nx, ny // 2, nz, CH, count), BF16),
                pltpu.VMEM((nx, ny // 2, nz, CH, count), BF16),
                pltpu.VMEM((members, 2, CH, width), BF16),
                pltpu.VMEM((members, 2, CH, width), BF16),
                pltpu.VMEM((members, 2, CH, width), BF16),
                pltpu.VMEM((members, 2, CH, width), BF16),
                pltpu.VMEM((quer, span), BF16),
                pltpu.VMEM((tall, quer), BF16),
                pltpu.VMEM((width, 2 * width), BF16),
                pltpu.VMEM((width, 2 * width), BF16),
                pltpu.VMEM((2, nx * tall, width), BF16),
                pltpu.VMEM((CH, count), F32),
                dma((2,)), dma((3,)), dma((2,)), dma((2, 2)),
                dma((2,)), dma((2, 8)), dma((2,)), dma((2, 4)),
            ],
            compiler_params=pltpu.CompilerParams(
                collective_id=0, has_side_effects=True, vmem_limit_bytes=60 * 1024 * 1024
            ),
        )(
            pair, token_mask.reshape(1, count), sg.reshape(1, width), sp, sb.T, so,
            eg.reshape(1, width), ep, eb.T, eo,
        )

    return jax.shard_map(
        body,
        mesh=mesh,
        in_specs=(P(("rep", "row"), None, None), P("rep"), P(), P(), P(), P(), P(), P(), P(), P()),
        out_specs=P(("rep", "row"), None, None),
        check_vma=False,
    )
```

```python
import functools
import math

import jax
import jax.numpy as jnp
from jax import lax
from jax.experimental import pallas as pl
from jax.experimental.pallas import tpu as pltpu
from jax.sharding import PartitionSpec as P

MESH = pl.DeviceIdType.MESH
LOG2E = 1.4426950408889634
F32 = jnp.float32
BF16 = jnp.bfloat16
ROWS = 4
TEAM = 2 * ROWS
HEADS = 4
CH = ROWS * HEADS


def iota(shape, dim):
    return lax.broadcasted_iota(jnp.int32, shape, dim)


def one_hot(cond):
    return cond.astype(F32).astype(BF16)


def nt(a, b):
    return lax.dot_general(a, b, (((1,), (1,)), ((), ())), preferred_element_type=F32)


def mm(a, b):
    return jnp.dot(a, b, preferred_element_type=F32)


def ln(wide, gain):
    center = wide - jnp.mean(wide, axis=-1, keepdims=True)
    spread = jnp.mean(center * center, axis=-1, keepdims=True)
    return (center * lax.rsqrt(spread + 1e-05) * gain).astype(BF16)


def kernel(
    dims,
    pair_in, mask_in, sg_in, sp_in, sb_in, so_in, eg_in, ep_in, eb_in, eo_in,
    out_ref,
    mask_ref, sg_ref, sp_ref, sb_ref, so_ref, eg_ref, ep_ref, eb_ref, eo_ref, load_sem,
    raw0_s, raw1_s, x_s, v_s, score_s, gate_s, res_s, e_s, top_s, low_s, turn_s,
    bias0_s, bias1_s, stage0_s, stage1_s, recv0_s, recv1_s, pick_s, spread_s, wkv_s, wqg_s, q_s, mask_s, total_s,
    t_send, t_recv, z_send, z_recv, x_send, x_recv, a_send, a_recv,
):
    nx, ny, nz = dims
    nyi, nzh = ny // 2, nz // 2
    near = nyi * nzh
    per = 2 * near
    members = nx * per
    me = lax.axis_index("row")
    x, y, z = me // (ny * nz), (me // nz) % ny, me % nz
    cls, yi = y % 2, y // 2
    hz, local = z // nzh, yi * nzh + z % nzh
    mine = (x * nyi + yi) * nz + z
    width = x_s.shape[2]
    count = x_s.shape[1]
    size = width // HEADS
    quer = per * ROWS
    tall = quer * HEADS
    span = per * TEAM
    group = nz * TEAM

    own = ROWS * cls
    other = ROWS - own
    own_rows = raw0_s.at[pl.ds(own, ROWS)]
    loads = (
        (pair_in, own_rows), (sg_in, sg_ref), (sb_in, sb_ref), (mask_in, mask_ref),
        (sp_in, sp_ref), (so_in, so_ref), (eg_in, eg_ref), (ep_in, ep_ref), (eb_in, eb_ref),
        (eo_in, eo_ref),
    )
    loads = [pltpu.make_async_copy(a, b, load_sem.at[i]) for i, (a, b) in enumerate(loads)]
    for load in loads:
        load.start()

    barrier = pltpu.get_barrier_semaphore()

    def greet_one(peer):
        pl.semaphore_signal(barrier, inc=1, device_id={"row": peer}, device_id_type=MESH)

    def member(m):
        return (2 * (m // nz) + cls) * nz + m % nz

    def place(p, half, i):
        return (p * nyi + i // nzh) * nz + half * nzh + i % nzh

    partner = me + nz * (1 - 2 * cls)
    greet_one(partner)

    def greet(s, c):
        greet_one(member(lax.rem(mine + s, members)))
        return c

    lax.fori_loop(1, members, greet, 0)

    def remote(src, dst, send, recv, peer):
        return pltpu.make_async_remote_copy(
            src_ref=src, dst_ref=dst, send_sem=send, recv_sem=recv,
            device_id={"row": peer}, device_id_type=MESH,
        )

    def wait_for(view, sem):
        pltpu.make_async_copy(view, view, sem).wait()

    def given(token):
        rest = token % span
        share = rest % quer // ROWS
        line = share // nz * group + share % nz * ROWS + rest % ROWS
        return token - rest + line + rest // quer * (nz * ROWS)

    lane_head = iota((quer, width), 1) // size
    head = (iota((tall, width), 0) % HEADS == iota((tall, width), 1) // size).astype(F32)
    far_mask = 1e9 * LOG2E

    up, down, far = lax.rem(x + 1, nx), lax.rem(x + nx - 1, nx), lax.rem(x + 2, nx)
    to_up = member(mine + (up - x) * per)
    to_down = member(mine + (down - x) * per)

    def part_of(bias, p, late):
        half = (hz + late) % 2
        return bias.at[p, :, pl.ds(half * nzh, nzh)]

    def quarter(bias, p, i, late):
        half = (hz + late) % 2
        return bias.at[p, i, pl.ds(half * nzh, nzh)]

    def head_rows(b_ref, r):
        a, b = iota((CH, HEADS), 0), iota((CH, HEADS), 1)
        return mm(one_hot((a // HEADS == r) & (a % HEADS == b)), b_ref[...]).astype(BF16)

    def gather_plane(t, bias):
        for late in range(2):

            def go(s, c):
                peer = member(place(x, (hz + late) % 2, lax.rem(local + s, near)))
                share = bias.at[x, yi, z]
                remote(share, share, z_send.at[t], z_recv.at[t, late], peer).start()
                return c

            lax.fori_loop(1 - late, near, go, 0)

    def to_neighbours(t, bias, late):
        part = part_of(bias, x, late)
        remote(part, part, x_send.at[t], x_recv.at[t, late], to_down).start()
        remote(part, part, x_send.at[t], x_recv.at[t, 2 + late], to_up).start()

    def relay(t, bias, late):
        wait_for(part_of(bias, up, late), x_recv.at[t, late])
        part = quarter(bias, up, 0, late)
        remote(part, part, x_send.at[t], x_recv.at[t, 4 + late], to_down).start()
        wait_for(part_of(bias, down, late), x_recv.at[t, 2 + late])
        part = quarter(bias, down, 1, late)
        remote(part, part, x_send.at[t], x_recv.at[t, 6 + late], to_up).start()

    def from_far(t, bias, late):
        wait_for(quarter(bias, far, 0, late), x_recv.at[t, 4 + late])
        wait_for(quarter(bias, far, 1, late), x_recv.at[t, 6 + late])

    def constants(t, p_ref):
        row, col = iota((quer, span), 0), iota((quer, span), 1)
        token = cls * quer + row
        pick_s[...] = one_hot((given(token) if t == 0 else token) == col)
        wkv_s[...] = p_ref[:, width : 3 * width]
        wqg_s[:, :width] = p_ref[:, :width]
        wqg_s[:, width:] = p_ref[:, 3 * width :]

    def update(t, g_ref, o_ref, raw, bias, stage, recv):
        def project(i):
            pair = (i, i + 1)
            kv = [mm(x_s[k], wkv_s[...]) for k in pair]
            keys = [a[:, :width].astype(BF16) for a in kv]
            for k, a in zip(pair, kv):
                v_s[k, :, :width] = a[:, width:].astype(BF16)
            for p in range(nx):
                part = slice(p * span, (p + 1) * span)
                both = jnp.concatenate(
                    [x_s[i, part, :], x_s[i + 1, part, :], raw[i, part, :], raw[i + 1, part, :]],
                    axis=1,
                )
                both = mm(pick_s[...], both)
                normed = both[:, : 2 * width].astype(BF16)
                normed = jnp.concatenate([normed[:, :width], normed[:, width:]], axis=0)
                qg = mm(normed, wqg_s[...])
                gate = jax.nn.sigmoid(qg[:, width:].astype(BF16).astype(F32))
                q = (qg[:, :width] * (LOG2E / math.sqrt(size))).astype(BF16)
                q = mm(spread_s[...], jnp.concatenate([q[:quer], q[quer:]], axis=1))
                for n, k in enumerate(pair):
                    res_s[k, p] = both[:, (2 + n) * width : (3 + n) * width]
                    gate_s[k, p] = gate[n * quer : (n + 1) * quer]
                    one = q[:, n * width : (n + 1) * width] * head
                    q_s[n, p * tall : (p + 1) * tall, :] = one.astype(BF16)
            for n, k in enumerate(pair):
                score_s[k] = nt(q_s[n], keys[n]).reshape(nx, tall, count)

        def finish(i):
            for k in (i, i + 1):
                x_s[k] = ln(raw[k].astype(F32), g_ref[...])
            project(i)

        project(own)
        project(own + 2)
        wait_for(bias.at[0, 0, pl.ds(0, near - 1)], z_recv.at[t, 0])
        to_neighbours(t, bias, 0)
        if t == 1:
            wait_for(raw.at[pl.ds(other, ROWS)], t_recv.at[2])
            finish(other)
        wait_for(part_of(bias, 0, 0), z_recv.at[t, 1])
        to_neighbours(t, bias, 1)
        if t == 1:
            finish(other + 2)

        def unit(n, c):
            if t == 0:
                rel = jnp.where(n < 6, n % 3, 3)
                kind = jnp.where(n < 6, n // 3, n % 2)

                @pl.when(n == 1)
                def _():
                    wait_for(raw.at[pl.ds(other, 2)], t_recv.at[0])
                    finish(other)
                    relay(t, bias, 0)
                    relay(t, bias, 1)

                @pl.when(n == 3)
                def _():
                    wait_for(raw.at[pl.ds(other + 2, 2)], t_recv.at[1])
                    finish(other + 2)

            else:
                rel, kind = n // 2, n % 2

                @pl.when(n == 2)
                def _():
                    relay(t, bias, 0)
                    relay(t, bias, 1)

            @pl.when(n == 6)
            def _():
                if t == 0:
                    for k in range(3):
                        arrive(k, 0)
                from_far(t, bias, 0)
                from_far(t, bias, 1)

            p = lax.rem(x + (rel ^ (rel >> 1)), nx)
            side = (cls + kind) % 2
            base = ROWS * side
            for r in range(ROWS):
                for k in range(per):
                    part = slice(k * CH, (k + 1) * CH)
                    add = bias[p, k // nz, k % nz].astype(F32)
                    s = score_s[base + r, p, part, :] + add
                    e_s[r, part, :] = jnp.exp2(s - jnp.max(s, axis=-1, keepdims=True)).astype(BF16)
                out = mm(e_s[r], v_s[base + r])
                top_s[r] = out[:, :width]
                low_s[r] = out[:, width:]
            hid = []
            for r in range(ROWS):
                top = top_s[r, pl.ds(0, quer, stride=HEADS), :]
                low = low_s[r, pl.ds(0, quer, stride=HEADS), :]
                for h in range(1, HEADS):
                    rows = pl.ds(h, quer, stride=HEADS)
                    top = jnp.where(lane_head == h, top_s[r, rows, :], top)
                    low = jnp.where(lane_head == h, low_s[r, rows, :], low)
                hid.append((gate_s[base + r, p] * (top / low)).astype(BF16))
            u = mm(jnp.concatenate(hid, axis=0), o_ref[...])
            if t == 1:
                u = u.astype(BF16).astype(F32)
            for r in range(ROWS):
                turn_s[pl.ds(r, quer, stride=ROWS), :] = (
                    res_s[base + r, p] + u[r * quer : (r + 1) * quer]
                )
            stage[pl.ds(p * per, per), side] = turn_s[...].astype(BF16).reshape(per, CH, width)

            def send(k):
                m = p * per + lax.rem(mine + k, per)
                remote(
                    stage.at[m, side], recv.at[mine, side], a_send.at[t], a_recv.at[t, 2 * rel + kind],
                    member(m),
                ).start()

            for k in range(1, per):
                send(k)

            @pl.when(rel == 0)
            def _():
                recv[mine, side] = stage[mine, side]

            @pl.when(rel > 0)
            def _():
                send(0)

            return c

        lax.fori_loop(0, 8, unit, 0)

    def taken(t, recv, n, kind):
        p, side = (x, down, up, far)[n], (cls + kind) % 2
        wait_for(recv.at[pl.ds(0, per - (n == 0)), 0], a_recv.at[t, 2 * n + kind])
        part = recv[pl.ds(p * per, per), side].reshape(per * CH, width)
        line = nz * CH
        part = [part[i * line : (i + 1) * line] for i in range(nyi)]
        o, i = iota((line, line), 0), iota((line, line), 1)
        rows = nz * ROWS
        order = one_hot(o % rows // ROWS * CH + o // rows * ROWS + o % ROWS == i)
        return p, side, mm(order, jnp.concatenate(part, axis=1))

    def arrive(n, kind):
        p, side, part = taken(0, recv0_s, n, kind)
        here = pl.ds(pl.multiple_of(p * span + side * quer, quer), quer)
        rows = nz * ROWS
        total = None
        for r in range(ROWS):
            row = part[r * rows : (r + 1) * rows]
            row = jnp.concatenate(
                [row[:, k * width : (k + 1) * width] for k in range(nyi)], axis=0
            )
            raw1_s[own + r, here, :] = row.astype(BF16)
            normed = ln(row, eg_ref[...])
            x_s[own + r, here, :] = normed
            term = nt(head_rows(eb_ref, r), normed)
            total = term if total is None else total + term
        total_s[n, kind] = total
        piece = raw1_s.at[pl.ds(own, ROWS), here, :]
        remote(piece, piece, t_send.at[1], t_recv.at[2], partner).start()

    def share_of_plane(n):
        p = (x, down, up, far)[n]
        here = pl.ds(pl.multiple_of(p * span, span), span)
        first, second = total_s[n, 0], total_s[n, 1]
        total = jnp.where(
            cls == 0,
            jnp.concatenate([first, second], axis=1),
            jnp.concatenate([second, first], axis=1),
        )
        bias1_s[x, yi, z, :, here] = (total * LOG2E + mask_s[:, here]).astype(BF16)

    def drain(t, raw, bias, stage):
        wait_for(raw.at[pl.ds(own, ROWS)], t_send.at[t])
        wait_for(bias.at[0, 0, pl.ds(0, near - 1)], z_send.at[t])
        wait_for(part_of(bias, 0, 0), z_send.at[t])
        wait_for(bias.at[pl.ds(0, 3)], x_send.at[t])
        wait_for(stage.at[pl.ds(0, members - 1)], a_send.at[t])

    for load in loads[:4]:
        load.wait()
    total = None
    for r in range(ROWS):
        normed = ln(raw0_s[own + r].astype(F32), sg_ref[...])
        x_s[own + r] = normed
        term = nt(head_rows(sb_ref, r), normed)
        total = term if total is None else total + term
    mask = mask_ref[...].astype(F32)
    bias0_s[x, yi, z] = (total * LOG2E + (mask - 1.0) * far_mask).astype(BF16)
    pl.semaphore_wait(barrier, members)
    gather_plane(0, bias0_s)
    for i in range(2):
        rows = raw0_s.at[pl.ds(own + 2 * i, 2)]
        remote(rows, rows, t_send.at[0], t_recv.at[i], partner).start()
    for load in loads[4:]:
        load.wait()
    v_s[:, :, width:] = jnp.ones((TEAM, count, width), BF16)
    spread_s[...] = one_hot(iota((tall, quer), 0) // HEADS == iota((tall, quer), 1))
    constants(0, sp_ref)

    update(0, sg_ref, so_ref, raw0_s, bias0_s, stage0_s, recv0_s)
    constants(1, ep_ref)
    order = one_hot(iota((count, count), 0) == given(iota((count, count), 1)))
    mask = mm(jnp.broadcast_to(mask_ref[...].astype(F32).astype(BF16), (CH, count)), order)
    mask_s[...] = (mask - 1.0) * far_mask
    for n in range(nx):
        if n == 3:
            arrive(n, 0)
        arrive(n, 1)
        share_of_plane(n)
    gather_plane(1, bias1_s)
    update(1, eg_ref, eo_ref, raw1_s, bias1_s, stage1_s, recv1_s)
    for n in range(nx):
        for kind in range(2):
            p, side, part = taken(1, recv1_s, n, kind)
            part = part.astype(BF16)
            rows = nz * ROWS
            for k in range(nyi):
                here = pl.ds(pl.multiple_of(p * span + k * group + side * rows, rows), rows)
                for r in range(ROWS):
                    out_ref[r, here, :] = part[
                        r * rows : (r + 1) * rows, k * width : (k + 1) * width
                    ]
    drain(0, raw0_s, bias0_s, stage0_s)
    drain(1, raw1_s, bias1_s, stage1_s)


def solution(mesh):
    n = mesh.shape["row"]
    dims = (4, 4, n // 16)

    def body(pair, token_mask, sg, sp, sb, so, eg, ep, eb, eo):
        rows, count, width = pair.shape
        nx, ny, nz = dims
        near, members = ny // 2 * (nz // 2), n // 2
        per = 2 * near
        quer, span = per * ROWS, per * TEAM
        tall = quer * HEADS
        vmem = pl.BlockSpec(memory_space=pltpu.VMEM)
        dma = pltpu.SemaphoreType.DMA
        return pl.pallas_call(
            functools.partial(kernel, dims),
            out_shape=jax.ShapeDtypeStruct(pair.shape, BF16),
            in_specs=[pl.BlockSpec(memory_space=pl.ANY)] * 10,
            out_specs=vmem,
            scratch_shapes=[
                pltpu.VMEM((1, count), jnp.int32),
                *[
                    shape
                    for _ in range(2)
                    for shape in (
                        pltpu.VMEM((1, width), F32),
                        pltpu.VMEM((width, 4 * width), BF16),
                        pltpu.VMEM((HEADS, width), BF16),
                        pltpu.VMEM((width, width), BF16),
                    )
                ],
                dma((10,)),
                pltpu.VMEM((TEAM, count, width), BF16),
                pltpu.VMEM((TEAM, count, width), BF16),
                pltpu.VMEM((TEAM, count, width), BF16),
                pltpu.VMEM((TEAM, count, 2 * width), BF16),
                pltpu.VMEM((TEAM, nx, tall, count), F32),
                pltpu.VMEM((TEAM, nx, quer, width), F32),
                pltpu.VMEM((TEAM, nx, quer, width), F32),
                pltpu.VMEM((ROWS, tall, count), BF16),
                pltpu.VMEM((ROWS, tall, width), F32),
                pltpu.VMEM((ROWS, tall, width), F32),
                pltpu.VMEM((quer * ROWS, width), F32),
                pltpu.VMEM((nx, ny // 2, nz, CH, count), BF16),
                pltpu.VMEM((nx, ny // 2, nz, CH, count), BF16),
                pltpu.VMEM((members, 2, CH, width), BF16),
                pltpu.VMEM((members, 2, CH, width), BF16),
                pltpu.VMEM((members, 2, CH, width), BF16),
                pltpu.VMEM((members, 2, CH, width), BF16),
                pltpu.VMEM((quer, span), BF16),
                pltpu.VMEM((tall, quer), BF16),
                pltpu.VMEM((width, 2 * width), BF16),
                pltpu.VMEM((width, 2 * width), BF16),
                pltpu.VMEM((2, nx * tall, width), BF16),
                pltpu.VMEM((CH, count), F32),
                pltpu.VMEM((nx, 2, CH, quer), F32),
                dma((2,)), dma((3,)), dma((2,)), dma((2, 2)),
                dma((2,)), dma((2, 8)), dma((2,)), dma((2, 8)),
            ],
            compiler_params=pltpu.CompilerParams(
                collective_id=0, has_side_effects=True, vmem_limit_bytes=60 * 1024 * 1024
            ),
        )(
            pair, token_mask.reshape(1, count), sg.reshape(1, width), sp, sb.T, so,
            eg.reshape(1, width), ep, eb.T, eo,
        )

    return jax.shard_map(
        body,
        mesh=mesh,
        in_specs=(P(("rep", "row"), None, None), P("rep"), P(), P(), P(), P(), P(), P(), P(), P()),
        out_specs=P(("rep", "row"), None, None),
        check_vma=False,
    )
```

```python
import functools
import math

import jax
import jax.numpy as jnp
from jax import lax
from jax.experimental import pallas as pl
from jax.experimental.pallas import tpu as pltpu
from jax.sharding import PartitionSpec as P

MESH = pl.DeviceIdType.MESH
LOG2E = 1.4426950408889634
F32 = jnp.float32
BF16 = jnp.bfloat16
ROWS = 4
TEAM = 2 * ROWS
HEADS = 4
CH = ROWS * HEADS


def iota(shape, dim):
    return lax.broadcasted_iota(jnp.int32, shape, dim)


def one_hot(cond):
    return cond.astype(F32).astype(BF16)


def nt(a, b):
    return lax.dot_general(a, b, (((1,), (1,)), ((), ())), preferred_element_type=F32)


def mm(a, b):
    return jnp.dot(a, b, preferred_element_type=F32)


def ln(wide, gain):
    center = wide - jnp.mean(wide, axis=-1, keepdims=True)
    spread = jnp.mean(center * center, axis=-1, keepdims=True)
    return (center * lax.rsqrt(spread + 1e-05) * gain).astype(BF16)


def kernel(
    dims,
    pair_in, mask_in, sg_in, sp_in, sb_in, so_in, eg_in, ep_in, eb_in, eo_in,
    out_ref,
    mask_ref, sg_ref, sp_ref, sb_ref, so_ref, eg_ref, ep_ref, eb_ref, eo_ref, load_sem,
    raw0_s, raw1_s, x_s, v_s, score_s, gate_s, res_s, e_s, top_s, low_s, turn_s,
    bias0_s, bias1_s, stage0_s, stage1_s, recv0_s, recv1_s, pick_s, spread_s, wkv_s, wqg_s, q_s, mask_s, total_s,
    t_send, t_recv, z_send, z_recv, x_send, x_recv, a_send, a_recv,
):
    nx, ny, nz = dims
    nyi, nzh = ny // 2, nz // 2
    near = nyi * nzh
    per = 2 * near
    members = nx * per
    me = lax.axis_index("row")
    x, y, z = me // (ny * nz), (me // nz) % ny, me % nz
    cls, yi = y % 2, y // 2
    hz, local = z // nzh, yi * nzh + z % nzh
    mine = (x * nyi + yi) * nz + z
    width = x_s.shape[2]
    count = x_s.shape[1]
    size = width // HEADS
    quer = per * ROWS
    tall = quer * HEADS
    span = per * TEAM
    group = nz * TEAM

    own = ROWS * cls
    other = ROWS - own
    own_rows = raw0_s.at[pl.ds(own, ROWS)]
    loads = (
        (pair_in, own_rows), (sg_in, sg_ref), (sb_in, sb_ref), (mask_in, mask_ref),
        (sp_in, sp_ref), (so_in, so_ref), (eg_in, eg_ref), (ep_in, ep_ref), (eb_in, eb_ref),
        (eo_in, eo_ref),
    )
    loads = [pltpu.make_async_copy(a, b, load_sem.at[i]) for i, (a, b) in enumerate(loads)]
    for load in loads:
        load.start()

    barrier = pltpu.get_barrier_semaphore()

    def greet_one(peer):
        pl.semaphore_signal(barrier, inc=1, device_id={"row": peer}, device_id_type=MESH)

    def member(m):
        return (2 * (m // nz) + cls) * nz + m % nz

    def place(p, half, i):
        return (p * nyi + i // nzh) * nz + half * nzh + i % nzh

    partner = me + nz * (1 - 2 * cls)
    greet_one(partner)

    along_z = [lax.rem(z + k, nz) for k in range(nz)]
    for i in range(nx):
        for j in range(nyi):
            line = (lax.rem(x + i, nx) * ny + 2 * lax.rem(yi + j, nyi) + cls) * nz
            for k in range(nz):
                if i + j + k > 0:
                    greet_one(line + along_z[k])

    def remote(src, dst, send, recv, peer):
        return pltpu.make_async_remote_copy(
            src_ref=src, dst_ref=dst, send_sem=send, recv_sem=recv,
            device_id={"row": peer}, device_id_type=MESH,
        )

    def wait_for(view, sem):
        pltpu.make_async_copy(view, view, sem).wait()

    def given(token):
        rest = token % span
        share = rest % quer // ROWS
        line = share // nz * group + share % nz * ROWS + rest % ROWS
        return token - rest + line + rest // quer * (nz * ROWS)

    lane_head = iota((quer, width), 1) // size
    head = (iota((tall, width), 0) % HEADS == iota((tall, width), 1) // size).astype(F32)
    far_mask = 1e9 * LOG2E

    up, down, far = lax.rem(x + 1, nx), lax.rem(x + nx - 1, nx), lax.rem(x + 2, nx)
    to_up = member(mine + (up - x) * per)
    to_down = member(mine + (down - x) * per)

    def part_of(bias, p, late):
        half = (hz + late) % 2
        return bias.at[p, :, pl.ds(half * nzh, nzh)]

    def quarter(bias, p, i, late):
        half = (hz + late) % 2
        return bias.at[p, i, pl.ds(half * nzh, nzh)]

    def head_rows(b_ref, r):
        a, b = iota((CH, HEADS), 0), iota((CH, HEADS), 1)
        return mm(one_hot((a // HEADS == r) & (a % HEADS == b)), b_ref[...]).astype(BF16)

    def gather_plane(t, bias):
        for late in range(2):

            for s in range(1 - late, near):
                peer = member(place(x, (hz + late) % 2, lax.rem(local + s, near)))
                share = bias.at[x, yi, z]
                remote(share, share, z_send.at[t], z_recv.at[t, late], peer).start()

    def to_neighbours(t, bias, late):
        part = part_of(bias, x, late)
        remote(part, part, x_send.at[t], x_recv.at[t, late], to_down).start()
        remote(part, part, x_send.at[t], x_recv.at[t, 2 + late], to_up).start()

    def relay(t, bias, late):
        wait_for(part_of(bias, up, late), x_recv.at[t, late])
        part = quarter(bias, up, 0, late)
        remote(part, part, x_send.at[t], x_recv.at[t, 4 + late], to_down).start()
        wait_for(part_of(bias, down, late), x_recv.at[t, 2 + late])
        part = quarter(bias, down, 1, late)
        remote(part, part, x_send.at[t], x_recv.at[t, 6 + late], to_up).start()

    def from_far(t, bias, late):
        wait_for(quarter(bias, far, 0, late), x_recv.at[t, 4 + late])
        wait_for(quarter(bias, far, 1, late), x_recv.at[t, 6 + late])

    def constants(t, p_ref):
        row, col = iota((quer, span), 0), iota((quer, span), 1)
        token = cls * quer + row
        pick_s[...] = one_hot((given(token) if t == 0 else token) == col)
        wkv_s[...] = p_ref[:, width : 3 * width]
        wqg_s[:, :width] = p_ref[:, :width]
        wqg_s[:, width:] = p_ref[:, 3 * width :]

    def update(t, g_ref, o_ref, raw, bias, stage, recv):
        def project(i):
            pair = (i, i + 1)
            kv = [mm(x_s[k], wkv_s[...]) for k in pair]
            keys = [a[:, :width].astype(BF16) for a in kv]
            for k, a in zip(pair, kv):
                v_s[k, :, :width] = a[:, width:].astype(BF16)
            for p in range(nx):
                part = slice(p * span, (p + 1) * span)
                both = jnp.concatenate(
                    [x_s[i, part, :], x_s[i + 1, part, :], raw[i, part, :], raw[i + 1, part, :]],
                    axis=1,
                )
                both = mm(pick_s[...], both)
                normed = both[:, : 2 * width].astype(BF16)
                normed = jnp.concatenate([normed[:, :width], normed[:, width:]], axis=0)
                qg = mm(normed, wqg_s[...])
                gate = jax.nn.sigmoid(qg[:, width:].astype(BF16).astype(F32))
                q = (qg[:, :width] * (LOG2E / math.sqrt(size))).astype(BF16)
                q = mm(spread_s[...], jnp.concatenate([q[:quer], q[quer:]], axis=1))
                for n, k in enumerate(pair):
                    res_s[k, p] = both[:, (2 + n) * width : (3 + n) * width]
                    gate_s[k, p] = gate[n * quer : (n + 1) * quer]
                    one = q[:, n * width : (n + 1) * width] * head
                    q_s[n, p * tall : (p + 1) * tall, :] = one.astype(BF16)
            for n, k in enumerate(pair):
                score_s[k] = nt(q_s[n], keys[n]).reshape(nx, tall, count)

        def finish(i):
            for k in (i, i + 1):
                x_s[k] = ln(raw[k].astype(F32), g_ref[...])
            project(i)

        project(own)
        project(own + 2)
        wait_for(bias.at[0, 0, pl.ds(0, near - 1)], z_recv.at[t, 0])
        to_neighbours(t, bias, 0)
        if t == 1:
            wait_for(raw.at[pl.ds(other, ROWS)], t_recv.at[2])
            finish(other)
        wait_for(part_of(bias, 0, 0), z_recv.at[t, 1])
        to_neighbours(t, bias, 1)
        if t == 1:
            finish(other + 2)

        def unit(n, c):
            if t == 0:
                rel = jnp.where(n < 6, n % 3, 3)
                kind = jnp.where(n < 6, n // 3, n % 2)

                @pl.when(n == 1)
                def _():
                    wait_for(raw.at[pl.ds(other, 2)], t_recv.at[0])
                    finish(other)
                    relay(t, bias, 0)
                    relay(t, bias, 1)

                @pl.when(n == 3)
                def _():
                    wait_for(raw.at[pl.ds(other + 2, 2)], t_recv.at[1])
                    finish(other + 2)

            else:
                rel, kind = n // 2, n % 2

                @pl.when(n == 2)
                def _():
                    relay(t, bias, 0)
                    relay(t, bias, 1)

            @pl.when(n == 6)
            def _():
                if t == 0:
                    for k in range(3):
                        arrive(k, 0)
                from_far(t, bias, 0)
                from_far(t, bias, 1)

            p = lax.rem(x + (rel ^ (rel >> 1)), nx)
            side = (cls + kind) % 2
            base = ROWS * side
            for r in range(ROWS):
                for k in range(per):
                    part = slice(k * CH, (k + 1) * CH)
                    add = bias[p, k // nz, k % nz].astype(F32)
                    s = score_s[base + r, p, part, :] + add
                    e_s[r, part, :] = jnp.exp2(s - jnp.max(s, axis=-1, keepdims=True)).astype(BF16)
                out = mm(e_s[r], v_s[base + r])
                top_s[r] = out[:, :width]
                low_s[r] = out[:, width:]
            hid = []
            for r in range(ROWS):
                top = top_s[r, pl.ds(0, quer, stride=HEADS), :]
                low = low_s[r, pl.ds(0, quer, stride=HEADS), :]
                for h in range(1, HEADS):
                    rows = pl.ds(h, quer, stride=HEADS)
                    top = jnp.where(lane_head == h, top_s[r, rows, :], top)
                    low = jnp.where(lane_head == h, low_s[r, rows, :], low)
                hid.append((gate_s[base + r, p] * (top / low)).astype(BF16))
            u = mm(jnp.concatenate(hid, axis=0), o_ref[...])
            if t == 1:
                u = u.astype(BF16).astype(F32)
            for r in range(ROWS):
                turn_s[pl.ds(r, quer, stride=ROWS), :] = (
                    res_s[base + r, p] + u[r * quer : (r + 1) * quer]
                )
            stage[pl.ds(p * per, per), side] = turn_s[...].astype(BF16).reshape(per, CH, width)

            def send(k):
                m = p * per + lax.rem(mine + k, per)
                remote(
                    stage.at[m, side], recv.at[mine, side], a_send.at[t], a_recv.at[t, 2 * rel + kind],
                    member(m),
                ).start()

            for k in range(1, per):
                send(k)

            @pl.when(rel == 0)
            def _():
                recv[mine, side] = stage[mine, side]

            @pl.when(rel > 0)
            def _():
                send(0)

            return c

        lax.fori_loop(0, 8, unit, 0)

    def taken(t, recv, n, kind):
        p, side = (x, down, up, far)[n], (cls + kind) % 2
        wait_for(recv.at[pl.ds(0, per - (n == 0)), 0], a_recv.at[t, 2 * n + kind])
        part = recv[pl.ds(p * per, per), side].reshape(per * CH, width)
        line = nz * CH
        part = [part[i * line : (i + 1) * line] for i in range(nyi)]
        o, i = iota((line, line), 0), iota((line, line), 1)
        rows = nz * ROWS
        order = one_hot(o % rows // ROWS * CH + o // rows * ROWS + o % ROWS == i)
        return p, side, mm(order, jnp.concatenate(part, axis=1))

    def arrive(n, kind):
        p, side, part = taken(0, recv0_s, n, kind)
        here = pl.ds(pl.multiple_of(p * span + side * quer, quer), quer)
        rows = nz * ROWS
        total = None
        for r in range(ROWS):
            row = part[r * rows : (r + 1) * rows]
            row = jnp.concatenate(
                [row[:, k * width : (k + 1) * width] for k in range(nyi)], axis=0
            )
            raw1_s[own + r, here, :] = row.astype(BF16)
            normed = ln(row, eg_ref[...])
            x_s[own + r, here, :] = normed
            term = nt(head_rows(eb_ref, r), normed)
            total = term if total is None else total + term
        total_s[n, kind] = total
        piece = raw1_s.at[pl.ds(own, ROWS), here, :]
        remote(piece, piece, t_send.at[1], t_recv.at[2], partner).start()

    def share_of_plane(n):
        p = (x, down, up, far)[n]
        here = pl.ds(pl.multiple_of(p * span, span), span)
        first, second = total_s[n, 0], total_s[n, 1]
        total = jnp.where(
            cls == 0,
            jnp.concatenate([first, second], axis=1),
            jnp.concatenate([second, first], axis=1),
        )
        bias1_s[x, yi, z, :, here] = (total * LOG2E + mask_s[:, here]).astype(BF16)

    def drain(t, raw, bias, stage):
        wait_for(raw.at[pl.ds(own, ROWS)], t_send.at[t])
        wait_for(bias.at[0, 0, pl.ds(0, near - 1)], z_send.at[t])
        wait_for(part_of(bias, 0, 0), z_send.at[t])
        wait_for(bias.at[pl.ds(0, 3)], x_send.at[t])
        wait_for(stage.at[pl.ds(0, members - 1)], a_send.at[t])

    for load in loads[:4]:
        load.wait()
    total = None
    for r in range(ROWS):
        normed = ln(raw0_s[own + r].astype(F32), sg_ref[...])
        x_s[own + r] = normed
        term = nt(head_rows(sb_ref, r), normed)
        total = term if total is None else total + term
    mask = mask_ref[...].astype(F32)
    bias0_s[x, yi, z] = (total * LOG2E + (mask - 1.0) * far_mask).astype(BF16)
    pl.semaphore_wait(barrier, members)
    gather_plane(0, bias0_s)
    for i in range(2):
        rows = raw0_s.at[pl.ds(own + 2 * i, 2)]
        remote(rows, rows, t_send.at[0], t_recv.at[i], partner).start()
    for load in loads[4:]:
        load.wait()
    v_s[:, :, width:] = jnp.ones((TEAM, count, width), BF16)
    spread_s[...] = one_hot(iota((tall, quer), 0) // HEADS == iota((tall, quer), 1))
    constants(0, sp_ref)

    update(0, sg_ref, so_ref, raw0_s, bias0_s, stage0_s, recv0_s)
    constants(1, ep_ref)
    order = one_hot(iota((count, count), 0) == given(iota((count, count), 1)))
    mask = mm(jnp.broadcast_to(mask_ref[...].astype(F32).astype(BF16), (CH, count)), order)
    mask_s[...] = (mask - 1.0) * far_mask
    for n in range(nx):
        if n == 3:
            arrive(n, 0)
        arrive(n, 1)
        share_of_plane(n)
    gather_plane(1, bias1_s)
    update(1, eg_ref, eo_ref, raw1_s, bias1_s, stage1_s, recv1_s)
    for n in range(nx):
        for kind in range(2):
            p, side, part = taken(1, recv1_s, n, kind)
            part = part.astype(BF16)
            rows = nz * ROWS
            for k in range(nyi):
                here = pl.ds(pl.multiple_of(p * span + k * group + side * rows, rows), rows)
                for r in range(ROWS):
                    out_ref[r, here, :] = part[
                        r * rows : (r + 1) * rows, k * width : (k + 1) * width
                    ]
    drain(0, raw0_s, bias0_s, stage0_s)
    drain(1, raw1_s, bias1_s, stage1_s)


def solution(mesh):
    n = mesh.shape["row"]
    dims = (4, 4, n // 16)

    def body(pair, token_mask, sg, sp, sb, so, eg, ep, eb, eo):
        rows, count, width = pair.shape
        nx, ny, nz = dims
        near, members = ny // 2 * (nz // 2), n // 2
        per = 2 * near
        quer, span = per * ROWS, per * TEAM
        tall = quer * HEADS
        vmem = pl.BlockSpec(memory_space=pltpu.VMEM)
        dma = pltpu.SemaphoreType.DMA
        return pl.pallas_call(
            functools.partial(kernel, dims),
            out_shape=jax.ShapeDtypeStruct(pair.shape, BF16),
            in_specs=[pl.BlockSpec(memory_space=pl.ANY)] * 10,
            out_specs=vmem,
            scratch_shapes=[
                pltpu.VMEM((1, count), jnp.int32),
                *[
                    shape
                    for _ in range(2)
                    for shape in (
                        pltpu.VMEM((1, width), F32),
                        pltpu.VMEM((width, 4 * width), BF16),
                        pltpu.VMEM((HEADS, width), BF16),
                        pltpu.VMEM((width, width), BF16),
                    )
                ],
                dma((10,)),
                pltpu.VMEM((TEAM, count, width), BF16),
                pltpu.VMEM((TEAM, count, width), BF16),
                pltpu.VMEM((TEAM, count, width), BF16),
                pltpu.VMEM((TEAM, count, 2 * width), BF16),
                pltpu.VMEM((TEAM, nx, tall, count), F32),
                pltpu.VMEM((TEAM, nx, quer, width), F32),
                pltpu.VMEM((TEAM, nx, quer, width), F32),
                pltpu.VMEM((ROWS, tall, count), BF16),
                pltpu.VMEM((ROWS, tall, width), F32),
                pltpu.VMEM((ROWS, tall, width), F32),
                pltpu.VMEM((quer * ROWS, width), F32),
                pltpu.VMEM((nx, ny // 2, nz, CH, count), BF16),
                pltpu.VMEM((nx, ny // 2, nz, CH, count), BF16),
                pltpu.VMEM((members, 2, CH, width), BF16),
                pltpu.VMEM((members, 2, CH, width), BF16),
                pltpu.VMEM((members, 2, CH, width), BF16),
                pltpu.VMEM((members, 2, CH, width), BF16),
                pltpu.VMEM((quer, span), BF16),
                pltpu.VMEM((tall, quer), BF16),
                pltpu.VMEM((width, 2 * width), BF16),
                pltpu.VMEM((width, 2 * width), BF16),
                pltpu.VMEM((2, nx * tall, width), BF16),
                pltpu.VMEM((CH, count), F32),
                pltpu.VMEM((nx, 2, CH, quer), F32),
                dma((2,)), dma((3,)), dma((2,)), dma((2, 2)),
                dma((2,)), dma((2, 8)), dma((2,)), dma((2, 8)),
            ],
            compiler_params=pltpu.CompilerParams(
                collective_id=0, has_side_effects=True, vmem_limit_bytes=60 * 1024 * 1024
            ),
        )(
            pair, token_mask.reshape(1, count), sg.reshape(1, width), sp, sb.T, so,
            eg.reshape(1, width), ep, eb.T, eo,
        )

    return jax.shard_map(
        body,
        mesh=mesh,
        in_specs=(P(("rep", "row"), None, None), P("rep"), P(), P(), P(), P(), P(), P(), P(), P()),
        out_specs=P(("rep", "row"), None, None),
        check_vma=False,
    )
```
